128 devices in a mesh: dp: 16 (over x_lo, y, core), tensor: 8 (over x_hi, z).
Axes of the slice: x: 4 (x_hi: 2, x_lo: 2; x = x_hi * 2 + x_lo), y: 4, z: 4, core: 2. Of those that a mesh axis runs over, the one named last changes fastest.
Arguments:
- tokens: bfloat16 [16384, 1024], P(('dp', 'tensor')), may hold values from -6 to 6
- cotangent: bfloat16 [16384, 1024], P(('dp', 'tensor')), may hold values from -6 to 6
- w_qkv: bfloat16 [1, 1024, 3, 1024], P(None, None, None, 'tensor'), may hold values from -0.25 to 0.25
- qv_bias: float32 [1, 2, 1024], P(None, None, 'tensor'), may hold values from -1.8 to 1.8
- w_out: bfloat16 [1, 1024, 1024], P(None, 'tensor'), may hold values from -0.5 to 0.5
- w_fc1: bfloat16 [1, 1024, 4096], P(None, None, 'tensor'), may hold values from -0.1875 to 0.1875
- b_fc1: float32 [1, 4096], P(None, 'tensor'), may hold values from -1.8 to 1.8
- w_fc2: bfloat16 [1, 4096, 1024], P(None, 'tensor'), may hold values from -0.09375 to 0.09375
- norm_gain: float32 [1, 2, 1024], replicated, may hold values from 0.1 to 1.9
- norm_shift: float32 [1, 2, 1024], replicated, may hold values from -1.8 to 1.8
- out_bias: float32 [1, 2, 1024], replicated, may hold values from -1.8 to 1.8
- layer_scale: float32 [1, 2, 1024], replicated, may hold values from 0.3 to 1.5
Outputs:
- activations: float32 [16384, 1024], P(('dp', 'tensor'))
- input_grad: float32 [16384, 1024], P(('dp', 'tensor'))
- grad_w_qkv: float32 [1, 1024, 3, 1024], P(None, None, None, 'tensor')
- grad_qv_bias: float32 [1, 2, 1024], P(None, None, 'tensor')
- grad_w_out: float32 [1, 1024, 1024], P(None, 'tensor')
- grad_w_fc1: float32 [1, 1024, 4096], P(None, None, 'tensor')
- grad_b_fc1: float32 [1, 4096], P(None, 'tensor')
- grad_w_fc2: float32 [1, 4096, 1024], P(None, 'tensor')
- grad_norm_gain: float32 [1, 2, 1024], replicated
- grad_norm_shift: float32 [1, 2, 1024], replicated
- grad_out_bias: float32 [1, 2, 1024], replicated
- grad_layer_scale: float32 [1, 2, 1024], replicated
The draws below stay inside these ranges and needn't reach their ends.
All inputs are finite; a program needn't handle non-finite values.
Results may differ from the reference program's by a relative error of at most 0.012.
The reference program's roundings to bfloat16 on the way count: a program that leaves them out, or rounds other values in their place, can miss the bound.
Values may be sent and summed in bfloat16 or wider, within the bound.
No kernel may reach another device: no remote copies, remote signals or barrier semaphores. Data moves between devices by JAX's collectives and lax.ppermute only.
A program may use at most 128 MiB of HBM per device.

```python
import math
import jax
import jax.numpy as jnp
from jax import lax

D = 1024
HEADS = 16
FF = 4096
HD = 64
SEQ = 1024
LAYERS = 1
TOKENS = 16384


def levels(stream_key, shape, split, smallest, top_value):
    def one(dim, shards_of):
        heights = jax.random.uniform(jax.random.fold_in(jax.random.fold_in(stream_key, 6), dim), (shards_of,), jnp.float32, smallest / len(split), top_value / len(split))
        return jnp.repeat(jnp.exp(heights), shape[dim] // shards_of).reshape((-1,) + (1,) * (len(shape) - dim - 1))

    factor_of = one(*split[0])
    for cut in split[1:]:
        factor_of = factor_of * one(*cut)
    return factor_of


def gaussian(stream_key, dims, width, bound, shards=(), kind=jnp.bfloat16):
    values = width * jax.random.normal(stream_key, dims, jnp.float32)
    if shards:
        values = values * levels(stream_key, dims, shards, -0.22, 0.18)
    return jnp.clip(values, -bound, bound).astype(kind)


def setup_inputs(seed: int = 0) -> dict:
    splits = jax.random.split(jax.random.key(seed), 13)
    tokens = gaussian(splits[0], (TOKENS, D), 1.0, 6.0, ((0, 128),))
    cotangent = gaussian(splits[1], (TOKENS, D), 1.0, 6.0, ((0, 128),))
    w_qkv = gaussian(splits[2], (LAYERS, D, 3, D), (max(D // 2, 1)) ** -0.5, 0.25, ((3, 8),))
    qv_bias = gaussian(splits[3], (LAYERS, 2, D), 0.3, 1.8, ((2, 8),), jnp.float32)
    w_out = gaussian(splits[4], (LAYERS, D, D), (max(D // 8, 1)) ** -0.5, 0.5, ((1, 8),))
    w_fc1 = gaussian(splits[5], (LAYERS, D, FF), D ** -0.5, 0.1875, ((2, 8),))
    b_fc1 = gaussian(splits[6], (LAYERS, FF), 0.3, 1.8, ((1, 8),), jnp.float32)
    w_fc2 = gaussian(splits[7], (LAYERS, FF, D), FF ** -0.5, 0.09375, ((1, 8),))
    norm_gain = jnp.clip(1.0 + 0.18 * jax.random.normal(splits[8], (LAYERS, 2, D), jnp.float32), 0.1, 1.9)
    norm_shift = gaussian(splits[9], (LAYERS, 2, D), 0.3, 1.8, (), jnp.float32)
    out_bias = gaussian(splits[10], (LAYERS, 2, D), 0.3, 1.8, (), jnp.float32)
    layer_scale = jnp.clip(jnp.exp(jax.random.uniform(splits[11], (LAYERS, 2, D), jnp.float32, math.log(0.3), math.log(1.5))), 0.3, 1.5)
    return dict(tokens=tokens, cotangent=cotangent, w_qkv=w_qkv, qv_bias=qv_bias, w_out=w_out, w_fc1=w_fc1, b_fc1=b_fc1, w_fc2=w_fc2, norm_gain=norm_gain, norm_shift=norm_shift, out_bias=out_bias, layer_scale=layer_scale)


highest = lax.Precision.HIGHEST

@jax.custom_vjp
def low(v):
    return lax.optimization_barrier(v.astype(jnp.bfloat16)).astype(jnp.float32)

@jax.custom_vjp
def low_back(v):
    return v

def low_keep(v):
    return (low(v), None)

def low_pass(kept, grad):
    return (grad,)

def back_keep(v):
    return (v, None)

def back_low(kept, grad):
    return (low(grad),)
low.defvjp(low_keep, low_pass)
low_back.defvjp(back_keep, back_low)

def layer_norm(values, gain, shift):
    centred = values - lax.optimization_barrier(jnp.mean(values, -1, keepdims=True))
    return centred * lax.rsqrt(lax.optimization_barrier(jnp.mean(centred * centred, -1, keepdims=True)) + 1e-06) * gain + shift

def attend(pieces):
    queries, keyset, valueset = pieces
    scores = low_back(jnp.einsum('qhd,khd->hqk', queries, keyset, precision=highest) * HD ** (-0.5))
    probs = low(jax.nn.softmax(scores, axis=-1))
    return jnp.einsum('hqk,khd->qhd', probs, valueset, precision=highest)

def layer_block(state, w_qkv, qv_bias, w_out, w_fc1, b_fc1, w_fc2, gain, shift, bias, scale):
    normed = low(layer_norm(state, gain[0], shift[0]))
    queries = low(low_back(jnp.dot(normed, w_qkv[:, 0], precision=highest) + qv_bias[0]))
    keyset = low(low_back(jnp.dot(normed, w_qkv[:, 1], precision=highest)))
    valueset = low(low_back(jnp.dot(normed, w_qkv[:, 2], precision=highest) + qv_bias[1]))
    images = state.shape[0] // SEQ
    shape_four = (images, SEQ, HEADS, HD)
    mixed = lax.map(jax.checkpoint(attend), (queries.reshape(shape_four), keyset.reshape(shape_four), valueset.reshape(shape_four)))
    mixed = low(low_back(mixed.reshape(state.shape[0], D)))
    branch = low_back(jnp.dot(mixed, w_out, precision=highest) + bias[0])
    middle = state + scale[0] * branch
    normed_two = low(layer_norm(middle, gain[1], shift[1]))
    pre_act = low_back(jnp.dot(normed_two, w_fc1, precision=highest) + b_fc1)
    hidden = low(jax.nn.gelu(pre_act, approximate=False))
    branch_two = low_back(jnp.dot(hidden, w_fc2, precision=highest) + bias[1])
    return middle + scale[1] * branch_two

def reference(tokens, cotangent, w_qkv, qv_bias, w_out, w_fc1, b_fc1, w_fc2, norm_gain, norm_shift, out_bias, layer_scale):

    def forward(state, p_qkv, p_qv, p_out, p_fc1, p_b1, p_fc2, p_gain, p_shift, p_bias, p_scale):
        for layer in range(LAYERS):
            state = layer_block(state, p_qkv[layer], p_qv[layer], p_out[layer], p_fc1[layer], p_b1[layer], p_fc2[layer], p_gain[layer], p_shift[layer], p_bias[layer], p_scale[layer])
        return state
    result, pullback = jax.vjp(forward, tokens.astype(jnp.float32), w_qkv.astype(jnp.float32), qv_bias.astype(jnp.float32), w_out.astype(jnp.float32), w_fc1.astype(jnp.float32), b_fc1.astype(jnp.float32), w_fc2.astype(jnp.float32), norm_gain.astype(jnp.float32), norm_shift.astype(jnp.float32), out_bias.astype(jnp.float32), layer_scale.astype(jnp.float32))
    grads = pullback(cotangent.astype(jnp.float32))
    return (result, grads[0], grads[1], grads[2], grads[3], grads[4], grads[5], grads[6], grads[7], grads[8], grads[9], grads[10])
```

```python
import math

import jax
import jax.numpy as jnp
from jax import lax
from jax.sharding import PartitionSpec as P

HD = 64
SEQ = 1024


inv_root_two = 1.0 / math.sqrt(2.0)
inv_root_two_pi = 1.0 / math.sqrt(2.0 * math.pi)


def norm_rows(values, gain, shift):
    centred = values - jnp.mean(values, -1, keepdims=True)
    inv_dev = lax.rsqrt(jnp.mean(centred * centred, -1, keepdims=True) + 1e-06)
    normed = centred * inv_dev
    return (normed, inv_dev, normed * gain + shift)


def norm_back(upstream, normed, inv_dev, gain):
    scaled = upstream * gain
    return inv_dev * (
        scaled
        - jnp.mean(scaled, -1, keepdims=True)
        - normed * jnp.mean(scaled * normed, -1, keepdims=True)
    )


def gelu_slope(values):
    return (
        0.5 * (1.0 + lax.erf(values * inv_root_two))
        + values * jnp.exp(-0.5 * values * values) * inv_root_two_pi
    )


AXES = ("dp", "tensor")


def links(move):
    pairs = []
    for xh in range(2):
        for xl in range(2):
            for y in range(4):
                for z in range(4):
                    for core in range(2):
                        there = move(xh, xl, y, z, core)
                        if there is None:
                            continue
                        ph, pl_, py, pz, pc = there
                        pairs.append(
                            (
                                ((xl * 4 + y) * 2 + core) * 8 + xh * 4 + z,
                                ((pl_ * 4 + py % 4) * 2 + pc) * 8 + ph * 4 + pz % 4,
                            )
                        )
    return pairs


z_up = links(lambda xh, xl, y, z, c: (xh, xl, y, z + 1, c))
z_down = links(lambda xh, xl, y, z, c: (xh, xl, y, z - 1, c))
z_far = links(lambda xh, xl, y, z, c: (xh, xl, y, z + 2, c))
y_up = links(lambda xh, xl, y, z, c: (xh, xl, y + 1, z, c))
y_down = links(lambda xh, xl, y, z, c: (xh, xl, y - 1, z, c))
y_far = links(lambda xh, xl, y, z, c: (xh, xl, y + 2, z, c))
x_up = links(lambda xh, xl, y, z, c: ((xh + xl) % 2, 1 - xl, y, z, c))
x_down = links(lambda xh, xl, y, z, c: ((xh + xl + 1) % 2, 1 - xl, y, z, c))
x_far = links(lambda xh, xl, y, z, c: (1 - xh, xl, y, z, c))
x_near = links(lambda xh, xl, y, z, c: (xh, 1 - xl, y, z, c))
cores = links(lambda xh, xl, y, z, c: (xh, xl, y, z, 1 - c))
regroup = links(lambda xh, xl, y, z, c: (c, xl, y, z, xh))
home = links(lambda xh, xl, y, z, c: (c, xl, y, z, c) if xh != c else None)


def move(values, pairs):
    return lax.ppermute(values, AXES, pairs)


def ring_from(values, up, down, far):
    return [values, move(values, down), move(values, up), move(values, far)]


def spread(rows):
    half = jnp.concatenate(ring_from(rows, z_up, z_down, z_far), 0)
    return jnp.concatenate([half, move(half, cores)], 0)


def collect(partial):
    half = partial.shape[0] // 2
    mine = partial[:half] + move(partial[half:].astype(jnp.bfloat16), cores).astype(jnp.float32)
    blocks = mine.reshape(4, half // 4, -1)
    sent = blocks.astype(jnp.bfloat16)
    return (
        blocks[0]
        + move(sent[1], z_up).astype(jnp.float32)
        + move(sent[2], z_down).astype(jnp.float32)
        + move(sent[3], z_far).astype(jnp.float32)
    )


def columns_to_rows(values):
    half = values.shape[0] // 2
    width = values.shape[1]
    both = jnp.concatenate([values[:half], move(values[half:], cores)], 1)
    blocks = both.reshape(4, half // 4, 2 * width)
    got = [blocks[0], move(blocks[1], z_up), move(blocks[2], z_down), move(blocks[3], z_far)]
    got = [got[0], got[2], got[1], got[3]]
    return jnp.concatenate([g[:, :width] for g in got] + [g[:, width:] for g in got], 1)


def rows_to_columns(values):
    rows = values.shape[0]
    width = values.shape[1] // 8
    pieces = values.reshape(rows, 2, 4, width)
    blocks = [pieces[:, :, n].reshape(rows, 2 * width) for n in range(4)]
    got = [blocks[0], move(blocks[1], z_up), move(blocks[2], z_down), move(blocks[3], z_far)]
    got = jnp.concatenate([got[0], got[2], got[1], got[3]], 0)
    return jnp.concatenate([got[:, :width], move(got[:, width:], cores)], 0)


def sum_images(partial, place):
    y, x_hi, core = place
    rows, width = partial.shape
    quarter = rows // 4
    pick = lambda n: lax.dynamic_slice_in_dim(partial, ((y + n) % 4) * quarter, quarter, 0)
    low = lambda v: v.astype(jnp.bfloat16)
    wide = lambda v: v.astype(jnp.float32)
    total = (
        pick(0)
        + wide(move(low(pick(1)), y_up))
        + wide(move(low(pick(3)), y_down))
        + wide(move(low(pick(2)), y_far))
    )
    total = total + wide(move(low(total), home))
    total = low(total)
    total = low(wide(total) + wide(move(total, x_near)))
    at_home = x_hi == core
    half = quarter // 2
    mine = jnp.where(at_home, total[:half], move(total[half:], cores))
    got = jnp.stack(ring_from(mine, y_up, y_down, y_far), 1)
    other = move(got, cores)
    first = jnp.where(at_home, got, other)
    second = jnp.where(at_home, other, got)
    full = jnp.stack([first, second], 0)
    order = [0, 1, 3, 2]
    ordered = jnp.stack([full[:, :, order[n]] for n in range(4)], 0)
    doubled = jnp.concatenate([ordered, ordered], 0)
    turned = lax.dynamic_slice_in_dim(doubled, (4 - y) % 4, 4, 0)
    return turned.reshape(rows, width).astype(jnp.float32)


def sum_ring(values, up, down, far):
    here, above, below, across = ring_from(values, up, down, far)
    return (here + across) + (above + below)


def attend_rows(pieces):
    query_img, key_img, value_img = pieces
    scores = jnp.einsum(
        "qhd,khd->hqk", query_img, key_img, preferred_element_type=jnp.float32
    ) * HD ** (-0.5)
    row_max = jnp.max(scores, -1, keepdims=True)
    shifted = jnp.exp(scores - row_max)
    row_total = jnp.sum(shifted, -1, keepdims=True)
    prob_low = (shifted / row_total).astype(jnp.bfloat16)
    result = jnp.einsum("hqk,khd->qhd", prob_low, value_img, preferred_element_type=jnp.float32)
    return (result.astype(jnp.bfloat16), (row_max + jnp.log(row_total))[..., 0])


def attend_back(pieces):
    query_img, key_img, value_img, grad_img, log_img = pieces
    scores = jnp.einsum(
        "qhd,khd->hqk", query_img, key_img, preferred_element_type=jnp.float32
    ) * HD ** (-0.5)
    probs = jnp.exp(scores - log_img[..., None])
    prob_low = probs.astype(jnp.bfloat16)
    value_grad = jnp.einsum("hqk,qhd->khd", prob_low, grad_img, preferred_element_type=jnp.float32)
    prob_grad = jnp.einsum("qhd,khd->hqk", grad_img, value_img, preferred_element_type=jnp.float32)
    score_grad = (probs * (prob_grad - jnp.sum(prob_grad * probs, -1, keepdims=True))).astype(
        jnp.bfloat16
    )
    query_grad = jnp.einsum(
        "hqk,khd->qhd", score_grad, key_img, preferred_element_type=jnp.float32
    ) * HD ** (-0.5)
    key_grad = jnp.einsum(
        "hqk,qhd->khd", score_grad, query_img, preferred_element_type=jnp.float32
    ) * HD ** (-0.5)
    return (
        query_grad.astype(jnp.bfloat16),
        key_grad.astype(jnp.bfloat16),
        value_grad.astype(jnp.bfloat16),
    )


def shards(
    tokens,
    cotangent,
    w_qkv,
    qv_bias,
    w_out,
    w_fc1,
    b_fc1,
    w_fc2,
    norm_gain,
    norm_shift,
    out_bias,
    layer_scale,
):
    layer = 0
    group = lax.axis_index("dp")
    core = group % 2
    y = (group // 2) % 4
    x_hi = lax.axis_index("tensor") // 4
    place = (y, x_hi, core)
    width = w_qkv.shape[3]
    heads_here = width // HD
    hidden_here = w_fc1.shape[2]

    rows_in = move(tokens, regroup)
    qkv_in = move(w_qkv[layer], regroup)
    grad_in = move(cotangent, regroup)
    fc1_in = move(w_fc1[layer], regroup)
    fc2_in = move(w_fc2[layer], regroup)
    out_in = move(w_out[layer], regroup)
    biases = move(
        jnp.concatenate([qv_bias[layer].reshape(1, -1), b_fc1], 1), regroup
    )
    q_bias = biases[0, :width]
    v_bias = biases[0, width : 2 * width]
    hidden_bias = biases[0, 2 * width :]

    tokens_full = spread(rows_in)
    rows_all = tokens_full.shape[0]
    normed_all, inv_all, shifted_all = norm_rows(
        tokens_full.astype(jnp.float32), norm_gain[layer, 0], norm_shift[layer, 0]
    )
    normed_full = shifted_all.astype(jnp.bfloat16)
    own = tokens.shape[0]
    state = rows_in.astype(jnp.float32)
    normed, inv_dev = normed_all[:own], inv_all[:own]
    projected = jnp.einsum("gd,dtc->gtc", normed_full, qkv_in, preferred_element_type=jnp.float32)
    shape_three = (rows_all, heads_here, HD)
    query_rows = (projected[:, 0] + q_bias).astype(jnp.bfloat16).reshape(shape_three)
    key_rows = projected[:, 1].astype(jnp.bfloat16).reshape(shape_three)
    value_rows = (projected[:, 2] + v_bias).astype(jnp.bfloat16).reshape(shape_three)
    mixed, log_total = attend_rows((query_rows, key_rows, value_rows))
    mixed = mixed.reshape(rows_all, width)
    out_full = spread(out_in)
    mixed_own = columns_to_rows(mixed)
    branch = (
        jnp.dot(mixed_own, out_full, preferred_element_type=jnp.float32) + out_bias[layer, 0]
    )
    middle = state + layer_scale[layer, 0] * branch
    normed_two, inv_two, shifted_two = norm_rows(middle, norm_gain[layer, 1], norm_shift[layer, 1])
    normed_two_full = spread(shifted_two.astype(jnp.bfloat16))

    gradient = grad_in.astype(jnp.float32)
    down_grad = (layer_scale[layer, 1] * gradient).astype(jnp.bfloat16)
    bias_two = jnp.sum(down_grad.astype(jnp.float32), 0)
    down_full = spread(down_grad)

    pre_act = (
        jnp.dot(normed_two_full, fc1_in, preferred_element_type=jnp.float32) + hidden_bias
    )
    hidden = jax.nn.gelu(pre_act, approximate=False).astype(jnp.bfloat16)
    hidden_grad = jnp.einsum("gd,fd->gf", down_full, fc2_in, preferred_element_type=jnp.float32)
    act_grad = (hidden_grad * gelu_slope(pre_act)).astype(jnp.bfloat16)
    rows_two = collect(
        jnp.einsum("gf,df->gd", act_grad, fc1_in, preferred_element_type=jnp.float32)
    )
    branch_two = (
        collect(jnp.dot(hidden, fc2_in, preferred_element_type=jnp.float32))
        + out_bias[layer, 1]
    )
    state_out = move(middle + layer_scale[layer, 1] * branch_two, regroup)
    scale_two = jnp.sum(gradient * branch_two, 0)
    grad_b1 = jnp.sum(act_grad.astype(jnp.float32), 0)
    grad_fc2 = jnp.einsum("gf,gd->fd", hidden, down_full, preferred_element_type=jnp.float32)
    grad_fc1 = jnp.einsum(
        "gd,gf->df", normed_two_full, act_grad, preferred_element_type=jnp.float32
    )

    gain_two = jnp.sum(rows_two * normed_two, 0)
    shift_two = jnp.sum(rows_two, 0)
    gradient = gradient + norm_back(rows_two, normed_two, inv_two, norm_gain[layer, 1])
    scale_one = jnp.sum(gradient * branch, 0)
    attn_grad = (layer_scale[layer, 0] * gradient).astype(jnp.bfloat16)
    bias_one = jnp.sum(attn_grad.astype(jnp.float32), 0)
    mixed_grad = rows_to_columns(
        jnp.einsum("gd,cd->gc", attn_grad, out_full, preferred_element_type=jnp.float32).astype(
            jnp.bfloat16
        )
    )
    attn_full = spread(attn_grad)
    grad_out = jnp.einsum("gc,gd->cd", mixed, attn_full, preferred_element_type=jnp.float32)
    query_grad, key_grad, value_grad = attend_back(
        (query_rows, key_rows, value_rows, mixed_grad.reshape(shape_three), log_total)
    )
    query_grad = query_grad.reshape(rows_all, width)
    value_grad = value_grad.reshape(rows_all, width)
    stacked = jnp.stack([query_grad, key_grad.reshape(rows_all, width), value_grad], 1)
    partial_one = jnp.einsum("gtc,dtc->gd", stacked, qkv_in, preferred_element_type=jnp.float32)
    rows_one = collect(partial_one)
    gain_one = jnp.sum(partial_one * normed_all, 0)
    shift_one = jnp.sum(partial_one, 0)
    gradient = gradient + norm_back(rows_one, normed, inv_dev, norm_gain[layer, 0])
    gradient_out = move(gradient, regroup)
    grad_qkv = jnp.einsum("gd,gtc->dtc", normed_full, stacked, preferred_element_type=jnp.float32)

    model = tokens.shape[1]
    total_fc2 = sum_images(grad_fc2, place)
    total_fc1 = sum_images(grad_fc1, place)
    total_out = sum_images(grad_out, place)
    total_qkv = sum_images(grad_qkv.reshape(model, 3 * width), place)

    small = jnp.stack(
        [gain_one, gain_two, shift_one, shift_two, bias_one, bias_two, scale_one, scale_two]
    )
    small = small + move(small, cores)
    small = sum_ring(small, z_up, z_down, z_far)
    wide_bias = jnp.concatenate(
        [
            jnp.sum(query_grad.astype(jnp.float32), 0),
            jnp.sum(value_grad.astype(jnp.float32), 0),
            grad_b1,
            jnp.zeros((model - 2 * width - hidden_here,), jnp.float32),
        ]
    )
    small = jnp.concatenate([small, wide_bias[None]], 0)
    small = sum_ring(small, y_up, y_down, y_far)
    small = sum_ring(small, x_up, x_down, x_far)
    wide_bias = small[8:]
    wide_bias = jnp.where(x_hi == core, wide_bias, move(wide_bias, cores))
    return (
        state_out,
        gradient_out,
        total_qkv.reshape(1, model, 3, width),
        wide_bias[:, : 2 * width].reshape(1, 2, width),
        total_out[None],
        total_fc1[None],
        wide_bias[:, 2 * width : 2 * width + hidden_here],
        total_fc2[None],
        small[0:2][None],
        small[2:4][None],
        small[4:6][None],
        small[6:8][None],
    )


def solution(mesh):
    return jax.shard_map(
        shards,
        mesh=mesh,
        in_specs=(
            P(("dp", "tensor"), None),
            P(("dp", "tensor"), None),
            P(None, None, None, "tensor"),
            P(None, None, "tensor"),
            P(None, "tensor", None),
            P(None, None, "tensor"),
            P(None, "tensor"),
            P(None, "tensor", None),
            P(),
            P(),
            P(),
            P(),
        ),
        out_specs=(
            P(("dp", "tensor"), None),
            P(("dp", "tensor"), None),
            P(None, None, None, "tensor"),
            P(None, None, "tensor"),
            P(None, "tensor", None),
            P(None, None, "tensor"),
            P(None, "tensor"),
            P(None, "tensor", None),
            P(),
            P(),
            P(),
            P(),
        ),
        check_vma=False,
    )
```

```python
import jax
import jax.numpy as jnp
from jax import lax
from jax.experimental import pallas as pl
from jax.experimental.pallas import tpu as pltpu
from jax.sharding import PartitionSpec as P

HD = 64
BLOCK = 256
inv_root_two = 0.7071067811865476
inv_root_two_pi = 0.3989422804014327
f32 = jnp.float32
bf16 = jnp.bfloat16


def dot_nn(a, b):
    return lax.dot_general(a, b, (((1,), (0,)), ((), ())), preferred_element_type=f32)


def dot_nt(a, b):
    return lax.dot_general(a, b, (((1,), (1,)), ((), ())), preferred_element_type=f32)


def params():
    return pltpu.CompilerParams(vmem_limit_bytes=48 * 1024 * 1024)


def whole(shape):
    return pl.BlockSpec(shape, lambda i, *_: (0,) * len(shape))


def rows_of(width, block=BLOCK):
    return pl.BlockSpec((block, width), lambda i, *_: (i, 0))


def rows_in_order(width, blocks):
    return pl.BlockSpec((BLOCK, width), lambda i, core: ((i + core[0] * (blocks // 2)) % blocks, 0))


def norm_pieces(values):
    centred = values - jnp.mean(values, -1, keepdims=True)
    inv_dev = lax.rsqrt(jnp.mean(centred * centred, -1, keepdims=True) + 1e-06)
    return centred * inv_dev, inv_dev


def project_kernel(x_ref, gain_ref, shift_ref, w_ref, bias_ref, h_ref, q_ref, k_ref, v_ref):
    normed, _ = norm_pieces(x_ref[...].astype(f32))
    h = (normed * gain_ref[...] + shift_ref[...]).astype(bf16)
    h_ref[...] = h
    q_ref[...] = (dot_nn(h, w_ref[0]) + bias_ref[0:1, :]).astype(bf16)
    k_ref[...] = dot_nn(h, w_ref[1]).astype(bf16)
    v_ref[...] = (dot_nn(h, w_ref[2]) + bias_ref[1:2, :]).astype(bf16)


def project(x, gain, shift, w, bias):
    rows, model = x.shape
    width = w.shape[2]
    out = jax.ShapeDtypeStruct((rows, width), bf16)
    return pl.pallas_call(
        project_kernel,
        grid=(rows // BLOCK,),
        in_specs=[rows_of(model), whole((1, model)), whole((1, model)), whole(w.shape), whole(bias.shape)],
        out_specs=[rows_of(model)] + [rows_of(width)] * 3,
        out_shape=[jax.ShapeDtypeStruct((rows, model), bf16), out, out, out],
        compiler_params=params(),
        name="norm_project",
    )(x, gain, shift, w, bias)


def lane_mask(shape, head, dim):
    return (lax.broadcasted_iota(jnp.int32, shape, dim) // HD) == head


def only_head(values, head, dim=1):
    return jnp.where(lane_mask(values.shape, head, dim), values, jnp.zeros_like(values))


def attend_kernel(core_ref, q_ref, k_ref, v_ref, o_ref, lse_ref):
    q = q_ref[...] * jnp.asarray(HD**-0.5, bf16)
    v_t = v_ref[...].T
    total = None
    for head in range(q.shape[1] // HD):
        scores = dot_nt(k_ref[...], only_head(q, head))
        top = jnp.max(scores, 0, keepdims=True)
        shifted = jnp.exp(scores - top)
        row_sum = jnp.sum(shifted, 0, keepdims=True)
        prob = (shifted * (1.0 / row_sum)).astype(bf16)
        lse_ref[head : head + 1, :] = top + jnp.log(row_sum)
        piece = dot_nn(only_head(v_t, head, 0), prob)
        total = piece if total is None else total + piece
    o_ref[...] = total.astype(bf16).T


def attend(core, q, k, v):
    rows, width = q.shape
    heads = width // HD
    return pl.pallas_call(
        attend_kernel,
        grid_spec=pltpu.PrefetchScalarGridSpec(
            num_scalar_prefetch=1,
            grid=(rows // BLOCK,),
            in_specs=[rows_of(width), whole(k.shape), whole(v.shape)],
            out_specs=[
                rows_in_order(width, rows // BLOCK),
                pl.BlockSpec((heads, BLOCK), lambda i, *_: (0, i)),
            ],
        ),
        out_shape=[jax.ShapeDtypeStruct((rows, width), bf16), jax.ShapeDtypeStruct((heads, rows), f32)],
        compiler_params=params(),
        name="attend",
    )(core, q, k, v)


def attend_back_kernel(
    core_ref,
    q_ref,
    do_ref,
    lse_ref,
    k_ref,
    v_ref,
    dq_ref,
    dk_ref,
    dv_ref,
    sum_ref,
    dk_acc,
    dv_acc,
):
    step = pl.program_id(0)
    last = pl.num_programs(0) - 1
    scale = HD**-0.5

    @pl.when(step == 0)
    def _():
        dk_acc[...] = jnp.zeros_like(dk_acc)
        dv_acc[...] = jnp.zeros_like(dv_acc)
        sum_ref[...] = jnp.zeros_like(sum_ref)

    q = q_ref[...] * jnp.asarray(scale, bf16)
    do = do_ref[...]
    k_t = k_ref[...].T
    dq_t = None
    for head in range(q.shape[1] // HD):
        q_h = only_head(q, head)
        do_h = only_head(do, head)
        prob = jnp.exp(dot_nt(k_ref[...], q_h) - lse_ref[head : head + 1, :])
        d_prob = dot_nt(v_ref[...], do_h)
        row = jnp.sum(d_prob * prob, 0, keepdims=True)
        d_score = (prob * (d_prob - row)).astype(bf16)
        dv_acc[...] += dot_nn(prob.astype(bf16), do_h)
        dk_acc[...] += dot_nn(d_score, q_h)
        piece = dot_nn(only_head(k_t, head, 0), d_score)
        dq_t = piece if dq_t is None else dq_t + piece
    dq = (dq_t * scale).astype(bf16).T
    dq_ref[...] = dq
    sum_ref[0:1, :] += jnp.sum(dq.astype(f32), 0, keepdims=True)

    @pl.when(step == last)
    def _():
        dk_ref[...] = dk_acc[...].astype(bf16)
        dv = dv_acc[...].astype(bf16)
        dv_ref[...] = dv
        sum_ref[1:2, :] = jnp.sum(dv.astype(f32), 0, keepdims=True)


def attend_back(core, q, k, v, do, lse):
    rows, width = q.shape
    heads = width // HD
    out = jax.ShapeDtypeStruct((rows, width), bf16)
    return pl.pallas_call(
        attend_back_kernel,
        grid_spec=pltpu.PrefetchScalarGridSpec(
            num_scalar_prefetch=1,
            grid=(rows // BLOCK,),
            in_specs=[
                rows_of(width),
                rows_in_order(width, rows // BLOCK),
                pl.BlockSpec((heads, BLOCK), lambda i, *_: (0, i)),
                whole(k.shape),
                whole(v.shape),
            ],
            out_specs=[rows_of(width), whole(k.shape), whole(v.shape), whole((8, width))],
            scratch_shapes=[pltpu.VMEM((rows, width), f32), pltpu.VMEM((rows, width), f32)],
        ),
        out_shape=[out, out, out, jax.ShapeDtypeStruct((8, width), f32)],
        compiler_params=params(),
        name="attend_back",
    )(core, q, do, lse, k, v)


def hidden_kernel(core_ref, h_ref, g_ref, w1_ref, b1_ref, w2_ref, m_ref, du_ref, dh_ref, f_ref, sum_ref):
    step = pl.program_id(0)
    u = dot_nn(h_ref[...], w1_ref[...]) + b1_ref[...]
    phi = 0.5 * (1.0 + lax.erf(u * inv_root_two))
    m = (u * phi).astype(bf16)
    m_ref[...] = m
    dm = dot_nt(g_ref[...], w2_ref[...])
    du = (dm * (phi + u * jnp.exp(-0.5 * u * u) * inv_root_two_pi)).astype(bf16)
    du_ref[...] = du
    dh_ref[...] = dot_nt(du, w1_ref[...]).astype(bf16)
    f_ref[...] = dot_nn(m, w2_ref[...]).astype(bf16)

    @pl.when(step == 0)
    def _():
        sum_ref[...] = jnp.zeros_like(sum_ref)

    sum_ref[0:1, :] += jnp.sum(du.astype(f32), 0, keepdims=True)


def hidden_block(core, h, g, w1, b1, w2):
    rows, model = h.shape
    width = w1.shape[1]
    return pl.pallas_call(
        hidden_kernel,
        grid_spec=pltpu.PrefetchScalarGridSpec(
            num_scalar_prefetch=1,
            grid=(rows // BLOCK,),
            in_specs=[
                rows_of(model),
                rows_in_order(model, rows // BLOCK),
                whole(w1.shape),
                whole((1, width)),
                whole(w2.shape),
            ],
            out_specs=[
                rows_in_order(width, rows // BLOCK),
                rows_of(width),
                rows_of(model),
                rows_of(model),
                whole((8, width)),
            ],
        ),
        out_shape=[
            jax.ShapeDtypeStruct((rows, width), bf16),
            jax.ShapeDtypeStruct((rows, width), bf16),
            jax.ShapeDtypeStruct((rows, model), bf16),
            jax.ShapeDtypeStruct((rows, model), bf16),
            jax.ShapeDtypeStruct((8, width), f32),
        ],
        compiler_params=params(),
        name="hidden_block",
    )(core, h, g, w1, b1, w2)


def project_back_kernel(dq_ref, dk_ref, dv_ref, w_ref, x_ref, early_ref, lo_ref, hi_ref, sum_ref):
    step = pl.program_id(0)
    half = pl.num_programs(0) // 2
    dh = dot_nt(dq_ref[...], w_ref[0]) + dot_nt(dk_ref[...], w_ref[1]) + dot_nt(dv_ref[...], w_ref[2])
    normed, _ = norm_pieces(x_ref[...].astype(f32))

    @pl.when(step == 0)
    def _():
        sum_ref[...] = early_ref[...]

    @pl.when(step < half)
    def _():
        lo_ref[pl.ds(pl.multiple_of(step * BLOCK, BLOCK), BLOCK), :] = dh.astype(bf16)

    @pl.when(step >= half)
    def _():
        hi_ref[pl.ds(pl.multiple_of((step - half) * BLOCK, BLOCK), BLOCK), :] = dh.astype(bf16)

    sum_ref[0:1, :] += jnp.sum(dh * normed, 0, keepdims=True)
    sum_ref[1:2, :] += jnp.sum(dh, 0, keepdims=True)

    @pl.when(step == 2 * half - 1)
    def _():
        hi_ref[half * BLOCK :, :] = sum_ref[...].astype(bf16)


def project_back(dq, dk, dv, w, x, early):
    rows, model = x.shape
    width = dq.shape[1]
    lo = (rows // 2, model)
    hi = (rows // 2 + 16, model)
    return pl.pallas_call(
        project_back_kernel,
        grid=(rows // BLOCK,),
        in_specs=[rows_of(width)] * 3 + [whole(w.shape), rows_of(model), whole((16, model))],
        out_specs=[whole(lo), whole(hi)],
        out_shape=[jax.ShapeDtypeStruct(lo, bf16), jax.ShapeDtypeStruct(hi, bf16)],
        scratch_shapes=[pltpu.VMEM((16, model), f32)],
        compiler_params=params(),
        name="project_back",
    )(dq, dk, dv, w, x, early)


def norm_back(upstream, normed, inv_dev, gain):
    scaled = upstream * gain
    return inv_dev * (
        scaled
        - jnp.mean(scaled, -1, keepdims=True)
        - normed * jnp.mean(scaled * normed, -1, keepdims=True)
    )


AXES = ("dp", "tensor")


def members(key):
    found = {}
    for core in range(2):
        for z in range(4):
            for y in range(4):
                for xh in range(2):
                    for xl in range(2):
                        found.setdefault(key(xh, xl, y, z, core), []).append(
                            ((xl * 4 + y) * 2 + core) * 8 + xh * 4 + z
                        )
    return list(found.values())


def links(move):
    pairs = []
    for xh in range(2):
        for xl in range(2):
            for y in range(4):
                for z in range(4):
                    for core in range(2):
                        there = move(xh, xl, y, z, core)
                        if there is None:
                            continue
                        ph, pl_, py, pz, pc = there
                        pairs.append(
                            (
                                ((xl * 4 + y) * 2 + core) * 8 + xh * 4 + z,
                                ((pl_ * 4 + py % 4) * 2 + pc) * 8 + ph * 4 + pz % 4,
                            )
                        )
    return pairs


z_up = links(lambda xh, xl, y, z, c: (xh, xl, y, z + 1, c))
z_down = links(lambda xh, xl, y, z, c: (xh, xl, y, z - 1, c))
z_far = links(lambda xh, xl, y, z, c: (xh, xl, y, z + 2, c))
y_up = links(lambda xh, xl, y, z, c: (xh, xl, y + 1, z, c))
y_down = links(lambda xh, xl, y, z, c: (xh, xl, y - 1, z, c))
y_far = links(lambda xh, xl, y, z, c: (xh, xl, y + 2, z, c))
x_far = links(lambda xh, xl, y, z, c: (1 - xh, xl, y, z, c))
x_near = links(lambda xh, xl, y, z, c: (xh, 1 - xl, y, z, c))
cores = links(lambda xh, xl, y, z, c: (xh, xl, y, z, 1 - c))
regroup = links(lambda xh, xl, y, z, c: (c, xl, y, z, xh))
home = links(lambda xh, xl, y, z, c: (c, xl, y, z, c) if xh != c else None)
ring_z = members(lambda xh, xl, y, z, c: (xh, xl, y, c))
ring_y = members(lambda xh, xl, y, z, c: (xh, xl, z, c))
image = members(lambda xh, xl, y, z, c: (xh, xl, y))


def move(values, pairs):
    return lax.ppermute(values, AXES, pairs)


def exchange(values, groups):
    return lax.all_to_all(values, AXES, 0, 0, axis_index_groups=groups, tiled=True)


def gather(values, groups):
    return lax.all_gather(values, AXES, axis=0, axis_index_groups=groups, tiled=True)


def ring_from(values, up, down, far):
    return [values, move(values, down), move(values, up), move(values, far)]


def spread(rows):
    half = exchange(jnp.concatenate([rows] * 4, 0), ring_z)
    return jnp.concatenate([half, move(half, cores)], 0)


def wide(values):
    return values.astype(f32)


def low(values):
    return values.astype(bf16)


def turn(values, axis, start):
    return lax.dynamic_slice_in_dim(jnp.concatenate([values, values], axis), start % 4, 4, axis)


def collect(lo, hi):
    mine = low(wide(lo) + wide(move(hi, cores)))
    got = exchange(mine, ring_z).reshape(4, -1, mine.shape[1])
    return jnp.sum(wide(got), 0)


def at_home(here, there, home_here):
    return jnp.where(home_here, here, there), jnp.where(home_here, there, here)


def shards(
    tokens,
    cotangent,
    w_qkv,
    qv_bias,
    w_out,
    w_fc1,
    b_fc1,
    w_fc2,
    norm_gain,
    norm_shift,
    out_bias,
    layer_scale,
):
    layer = 0
    place = lax.axis_index("dp")
    core = place % 2
    y = (place // 2) % 4
    x_hi = lax.axis_index("tensor") // 4
    z = lax.axis_index("tensor") % 4
    home_here = x_hi == core
    core_arg = core.astype(jnp.int32).reshape(1)
    width = w_qkv.shape[3]
    hidden_here = w_fc1.shape[2]
    own, model = tokens.shape

    rows_in = move(tokens, regroup)
    qkv_in = move(jnp.moveaxis(w_qkv[layer], 1, 0), regroup)
    biases = move(jnp.concatenate([qv_bias[layer].reshape(1, -1), b_fc1], 1), regroup)
    out_in = move(w_out[layer], regroup)
    grad_in = move(cotangent, regroup)
    fc1_in = move(w_fc1[layer], regroup)
    fc2_in = move(w_fc2[layer], regroup)
    qv_in = biases[:, : 2 * width].reshape(2, width)
    hidden_bias = biases[:, 2 * width :]

    tokens_full = spread(rows_in)
    out_full = gather(out_in, image)
    normed_full, query_rows, key_rows, value_rows = project(
        tokens_full, norm_gain[layer, 0:1], norm_shift[layer, 0:1], qkv_in, qv_in
    )
    mixed, log_total = attend(core_arg, query_rows, key_rows, value_rows)
    state = wide(rows_in)
    normed, inv_dev = norm_pieces(state)

    gradient = wide(grad_in)
    down_grad = low(layer_scale[layer, 1] * gradient)
    bias_two = jnp.sum(wide(down_grad), 0)
    down_full = gather(down_grad, image)

    pieces = exchange(mixed, image).reshape(8, own, width)
    mixed_own = jnp.moveaxis(pieces, 0, 1).reshape(own, model)
    branch = jnp.dot(mixed_own, out_full, preferred_element_type=f32) + out_bias[layer, 0]
    middle = state + layer_scale[layer, 0] * branch
    normed_two, inv_two = norm_pieces(middle)
    shifted_two = normed_two * norm_gain[layer, 1] + norm_shift[layer, 1]
    normed_two_full = spread(low(shifted_two))

    hidden, act_grad, partial_two, partial_f, hidden_sums = hidden_block(
        core_arg, normed_two_full, down_full, fc1_in, hidden_bias, fc2_in
    )
    half = normed_two_full.shape[0] // 2
    rows_two = collect(partial_two[:half], partial_two[half:])
    grad_b1 = hidden_sums[0]

    grad_fc2 = jnp.einsum("gf,gd->fd", hidden, down_full, preferred_element_type=f32)
    grad_fc1 = jnp.einsum("gd,gf->df", normed_two_full, act_grad, preferred_element_type=f32)
    joined = jnp.concatenate(
        [low(grad_fc1), low(grad_fc2[:, : model // 2]), low(grad_fc2[:, model // 2 :])], 0
    )
    fc_quarter = lax.psum_scatter(
        joined, AXES, scatter_dimension=0, axis_index_groups=ring_y, tiled=True
    )
    fc_quarter = low(wide(fc_quarter) + wide(move(fc_quarter, home)))
    fc_quarter = low(wide(fc_quarter) + wide(move(fc_quarter, x_near)))
    fc_half = fc_quarter.shape[0] // 2
    fc_part = jnp.where(home_here, fc_quarter[:fc_half], move(fc_quarter[fc_half:], cores))
    fc_got = gather(fc_part, ring_y).reshape(4, fc_half, -1)
    fc_first, fc_second = at_home(fc_got, move(fc_got, cores), home_here)
    fc_total = wide(jnp.stack([fc_first, fc_second], 1).reshape(joined.shape))
    total_fc1 = fc_total[:model]
    total_fc2 = jnp.concatenate(
        [fc_total[model : model + hidden_here], fc_total[model + hidden_here :]], 1
    )

    gain_two = jnp.sum(rows_two * normed_two, 0)
    shift_two = jnp.sum(rows_two, 0)
    gradient_two = gradient + norm_back(rows_two, normed_two, inv_two, norm_gain[layer, 1])
    scale_one = jnp.sum(gradient_two * branch, 0)
    attn_grad = low(layer_scale[layer, 0] * gradient_two)
    bias_one = jnp.sum(wide(attn_grad), 0)
    mixed_grad = low(
        jnp.einsum("gd,cd->gc", attn_grad, out_full, preferred_element_type=f32)
    )
    mixed_grad = jnp.moveaxis(mixed_grad.reshape(own, 8, width), 1, 0).reshape(8 * own, width)
    mixed_grad = exchange(mixed_grad, image)

    f_mine = low(wide(partial_f[:half]) + wide(move(partial_f[half:], cores)))
    f_turned = turn(f_mine.reshape(4, own, model), 0, z)
    sent = [jnp.concatenate([f_turned[n], attn_grad], 0) for n in range(4)]
    got = [sent[0], move(sent[3], z_down), move(sent[1], z_up), move(sent[2], z_far)]
    branch_two = (
        wide(got[0][:own]) + wide(got[1][:own]) + wide(got[2][:own]) + wide(got[3][:own])
    ) + out_bias[layer, 1]
    attn_half = jnp.concatenate([piece[own:] for piece in got], 0)
    attn_full = jnp.concatenate([attn_half, move(attn_half, cores)], 0)
    mixed_turned = turn(mixed.reshape(2, 4, own, width), 1, z)
    mixed_first, mixed_second = at_home(mixed_turned[0], mixed_turned[1], core == 0)
    mixed_turned = jnp.stack([mixed_first, mixed_second])
    mixed_turned = jnp.stack([mixed_turned[:, n] for n in (0, 1, 3, 2)], 1)
    grad_out = jnp.einsum(
        "gc,gd->cd",
        mixed_turned.reshape(8 * own, width),
        attn_full,
        preferred_element_type=f32,
    )
    state_out = move(middle + layer_scale[layer, 1] * branch_two, regroup)
    scale_two = jnp.sum(gradient * branch_two, 0)

    query_grad, key_grad, value_grad, qv_sums = attend_back(
        core_arg, query_rows, key_rows, value_rows, mixed_grad, log_total
    )
    stacked = jnp.stack([query_grad, key_grad, value_grad])
    grad_qkv = low(jnp.einsum("gd,tgc->tdc", normed_full, stacked, preferred_element_type=f32))
    early = jnp.stack(
        [
            jnp.zeros_like(gain_two),
            jnp.zeros_like(gain_two),
            gain_two,
            shift_two,
            bias_one,
            bias_two,
            scale_one,
            scale_two,
        ]
    )
    early = jnp.concatenate([early, jnp.zeros_like(early)], 0)
    lo, hi = project_back(query_grad, key_grad, value_grad, qkv_in, tokens_full, early)

    payload = jnp.concatenate(
        [grad_qkv.reshape(3 * model, width), low(grad_out).reshape(model, width)], 0
    )
    quarter = payload.shape[0] // 4
    payload = turn(payload.reshape(4, quarter, width), 0, y)
    rows_q = (
        wide(payload[0])
        + wide(move(payload[1], y_up))
        + wide(move(payload[3], y_down))
        + wide(move(payload[2], y_far))
    )

    hi_got = move(hi, cores)
    mine = low(wide(lo) + wide(hi_got[:half])).reshape(4, own, model)
    small = low(wide(hi[half:]) + wide(hi_got[half:]))
    mine = jnp.concatenate([mine, jnp.broadcast_to(small[None], (4, 16, model))], 1)
    got = exchange(mine.reshape(-1, model), ring_z).reshape(4, own + 16, model)
    rows_one = jnp.sum(wide(got[:, :own]), 0)
    small = low(jnp.sum(wide(got[:, own : own + 8]), 0)).reshape(8 * model // width, width)
    gradient_one = gradient_two + norm_back(rows_one, normed, inv_dev, norm_gain[layer, 0])
    gradient_out = move(gradient_one, regroup)

    wide_bias = jnp.concatenate(
        [qv_sums[:2].reshape(-1), grad_b1, jnp.zeros((model - 2 * width - hidden_here,), f32)]
    )
    wide_bias = jnp.concatenate([wide_bias, jnp.zeros_like(wide_bias)]).reshape(-1, width)
    flow = jnp.concatenate([low(rows_q), small, low(wide_bias)], 0)
    flow = low(wide(flow) + wide(move(flow, x_far)))
    flow = low(wide(flow) + wide(move(flow, x_near)))
    fine = quarter // 2
    kept = jnp.where(home_here, flow[:fine], move(flow[fine:quarter], cores))
    here, above, below, across = ring_from(
        jnp.concatenate([kept, flow[quarter:]], 0), y_up, y_down, y_far
    )
    tail = (wide(here[fine:]) + wide(across[fine:])) + (wide(above[fine:]) + wide(below[fine:]))
    small_total = tail[: 8 * model // width].reshape(8, model)
    bias_mine = low(tail[8 * model // width :])
    block = jnp.concatenate([here[:fine], above[:fine], across[:fine], below[:fine], bias_mine], 0)
    other = move(block, cores)
    first, second = at_home(block, other, home_here)
    ordered = jnp.stack(
        [first[: 4 * fine].reshape(4, fine, width), second[: 4 * fine].reshape(4, fine, width)], 1
    )
    total = wide(turn(ordered, 0, 4 - y).reshape(4 * quarter, width))
    total_qkv = jnp.moveaxis(total[: 3 * model].reshape(3, model, width), 0, 1)
    total_out = total[3 * model :].reshape(width, model)
    bias_total = wide(first[4 * fine :]).reshape(2, model)[:1]
    return (
        state_out,
        gradient_out,
        total_qkv[None],
        bias_total[:, : 2 * width].reshape(1, 2, width),
        total_out[None],
        total_fc1[None],
        bias_total[:, 2 * width : 2 * width + hidden_here],
        total_fc2[None],
        jnp.stack([small_total[0], small_total[2]])[None],
        jnp.stack([small_total[1], small_total[3]])[None],
        small_total[4:6][None],
        small_total[6:8][None],
    )


def solution(mesh):
    return jax.shard_map(
        shards,
        mesh=mesh,
        in_specs=(
            P(("dp", "tensor"), None),
            P(("dp", "tensor"), None),
            P(None, None, None, "tensor"),
            P(None, None, "tensor"),
            P(None, "tensor", None),
            P(None, None, "tensor"),
            P(None, "tensor"),
            P(None, "tensor", None),
            P(),
            P(),
            P(),
            P(),
        ),
        out_specs=(
            P(("dp", "tensor"), None),
            P(("dp", "tensor"), None),
            P(None, None, None, "tensor"),
            P(None, None, "tensor"),
            P(None, "tensor", None),
            P(None, None, "tensor"),
            P(None, "tensor"),
            P(None, "tensor", None),
            P(),
            P(),
            P(),
            P(),
        ),
        check_vma=False,
    )
```

```python
import functools

import jax
import jax.numpy as jnp
from jax import lax
from jax.experimental import pallas as pl
from jax.experimental.pallas import tpu as pltpu
from jax.sharding import PartitionSpec as P

HD = 64
BLOCK = 256
inv_root_two = 0.7071067811865476
inv_root_two_pi = 0.3989422804014327
f32 = jnp.float32
bf16 = jnp.bfloat16


def dot_nn(a, b):
    return lax.dot_general(a, b, (((1,), (0,)), ((), ())), preferred_element_type=f32)


def dot_nt(a, b):
    return lax.dot_general(a, b, (((1,), (1,)), ((), ())), preferred_element_type=f32)


def params(mebibytes=24):
    return pltpu.CompilerParams(vmem_limit_bytes=mebibytes * 1024 * 1024)


def whole(shape):
    return pl.BlockSpec(shape, lambda i, *_: (0,) * len(shape))


def rows_of(width, block=BLOCK):
    return pl.BlockSpec((block, width), lambda i, *_: (i, 0))


def rows_in_order(width, blocks):
    return pl.BlockSpec((BLOCK, width), lambda i, core: ((i + core[0] * (blocks // 2)) % blocks, 0))


def half_specs(width, blocks):
    half = blocks // 2
    return [
        pl.BlockSpec((BLOCK, width), lambda i, *_: (jnp.minimum(i, half - 1), 0)),
        pl.BlockSpec((BLOCK, width), lambda i, *_: (jnp.maximum(i - half, 0), 0)),
    ]


def from_halves(lo_ref, hi_ref):
    return jnp.where(pl.program_id(0) < pl.num_programs(0) // 2, lo_ref[...], hi_ref[...])


def to_halves(values, lo_ref, hi_ref):
    step = pl.program_id(0)
    half = pl.num_programs(0) // 2

    @pl.when(step < half)
    def _():
        lo_ref[pl.ds(pl.multiple_of(step * BLOCK, BLOCK), BLOCK), :] = values

    @pl.when(step >= half)
    def _():
        hi_ref[pl.ds(pl.multiple_of((step - half) * BLOCK, BLOCK), BLOCK), :] = values


def norm_pieces(values):
    centred = values - jnp.mean(values, -1, keepdims=True)
    inv_dev = lax.rsqrt(jnp.mean(centred * centred, -1, keepdims=True) + 1e-06)
    return centred * inv_dev, inv_dev


def project_kernel(lo_ref, hi_ref, gain_ref, shift_ref, w_ref, bias_ref, h_ref, q_ref, k_ref, v_ref):
    normed, _ = norm_pieces(from_halves(lo_ref, hi_ref).astype(f32))
    h = (normed * gain_ref[...] + shift_ref[...]).astype(bf16)
    h_ref[...] = h
    q_ref[...] = (dot_nn(h, w_ref[0]) + bias_ref[0:1, :]).astype(bf16)
    k_ref[...] = dot_nn(h, w_ref[1]).astype(bf16)
    v_ref[...] = (dot_nn(h, w_ref[2]) + bias_ref[1:2, :]).astype(bf16)


def project(lo, hi, gain, shift, w, bias):
    rows, model = 2 * lo.shape[0], lo.shape[1]
    width = w.shape[2]
    out = jax.ShapeDtypeStruct((rows, width), bf16)
    return pl.pallas_call(
        project_kernel,
        grid=(rows // BLOCK,),
        in_specs=half_specs(model, rows // BLOCK)
        + [whole((1, model)), whole((1, model)), whole(w.shape), whole(bias.shape)],
        out_specs=[rows_of(model)] + [rows_of(width)] * 3,
        out_shape=[jax.ShapeDtypeStruct((rows, model), bf16), out, out, out],
        compiler_params=params(),
        name="norm_project",
    )(lo, hi, gain, shift, w, bias)


def lane_mask(shape, head, dim):
    return (lax.broadcasted_iota(jnp.int32, shape, dim) // HD) == head


def only_head(values, head, dim=1):
    return jnp.where(lane_mask(values.shape, head, dim), values, jnp.zeros_like(values))


def attend_kernel(core_ref, q_ref, k_ref, v_ref, o_ref, own_ref, lse_ref):
    q = q_ref[...] * jnp.asarray(HD**-0.5, bf16)
    v_t = v_ref[...].T
    total = None
    for head in range(q.shape[1] // HD):
        scores = dot_nt(k_ref[...], only_head(q, head))
        top = jnp.max(scores, 0, keepdims=True)
        shifted = jnp.exp(scores - top)
        row_sum = jnp.sum(shifted, 0, keepdims=True)
        prob = (shifted * (1.0 / row_sum)).astype(bf16)
        lse_ref[head : head + 1, :] = top + jnp.log(row_sum)
        piece = dot_nn(only_head(v_t, head, 0), prob)
        total = piece if total is None else total + piece
    o = total.astype(bf16).T
    o_ref[...] = o
    own_ref[...] = o


def attend(core, q, k, v):
    rows, width = q.shape
    heads = width // HD
    return pl.pallas_call(
        attend_kernel,
        grid_spec=pltpu.PrefetchScalarGridSpec(
            num_scalar_prefetch=1,
            grid=(rows // BLOCK,),
            in_specs=[rows_of(width), whole(k.shape), whole(v.shape)],
            out_specs=[
                rows_in_order(width, rows // BLOCK),
                rows_of(width),
                pl.BlockSpec((heads, BLOCK), lambda i, *_: (0, i)),
            ],
        ),
        out_shape=[jax.ShapeDtypeStruct((rows, width), bf16)] * 2 + [jax.ShapeDtypeStruct((heads, rows), f32)],
        compiler_params=params(),
        name="attend",
    )(core, q, k, v)


def attend_back_kernel(
    q_ref,
    do_lo_ref,
    do_hi_ref,
    lse_ref,
    k_ref,
    v_ref,
    dq_ref,
    dk_ref,
    dv_ref,
    sum_ref,
    dk_acc,
    dv_acc,
):
    step = pl.program_id(0)
    last = pl.num_programs(0) - 1
    scale = HD**-0.5

    @pl.when(step == 0)
    def _():
        dk_acc[...] = jnp.zeros_like(dk_acc)
        dv_acc[...] = jnp.zeros_like(dv_acc)
        sum_ref[...] = jnp.zeros_like(sum_ref)

    q = q_ref[...] * jnp.asarray(scale, bf16)
    do = from_halves(do_lo_ref, do_hi_ref)
    k_t = k_ref[...].T
    dq_t = None
    for head in range(q.shape[1] // HD):
        q_h = only_head(q, head)
        do_h = only_head(do, head)
        prob = jnp.exp(dot_nt(k_ref[...], q_h) - lse_ref[head : head + 1, :])
        d_prob = dot_nt(v_ref[...], do_h)
        row = jnp.sum(d_prob * prob, 0, keepdims=True)
        d_score = (prob * (d_prob - row)).astype(bf16)
        dv_acc[...] += dot_nn(prob.astype(bf16), do_h)
        dk_acc[...] += dot_nn(d_score, q_h)
        piece = dot_nn(only_head(k_t, head, 0), d_score)
        dq_t = piece if dq_t is None else dq_t + piece
    dq = (dq_t * scale).astype(bf16).T
    dq_ref[...] = dq
    sum_ref[0:1, :] += jnp.sum(dq.astype(f32), 0, keepdims=True)

    @pl.when(step == last)
    def _():
        dk_ref[...] = dk_acc[...].astype(bf16)
        dv = dv_acc[...].astype(bf16)
        dv_ref[...] = dv
        sum_ref[1:2, :] = jnp.sum(dv.astype(f32), 0, keepdims=True)


def attend_back(q, k, v, do_lo, lo_block, do_hi, hi_block, lse):
    rows, width = q.shape
    heads = width // HD
    half = rows // BLOCK // 2
    out = jax.ShapeDtypeStruct((rows, width), bf16)
    return pl.pallas_call(
        attend_back_kernel,
        grid=(rows // BLOCK,),
        in_specs=[
            rows_of(width),
            pl.BlockSpec((BLOCK, width), lambda i: (jnp.minimum(i, half - 1), lo_block)),
            pl.BlockSpec((BLOCK, width), lambda i: (jnp.maximum(i - half, 0), hi_block)),
            pl.BlockSpec((heads, BLOCK), lambda i: (0, i)),
            whole(k.shape),
            whole(v.shape),
        ],
        out_specs=[rows_of(width), whole(k.shape), whole(v.shape), whole((8, width))],
        out_shape=[out, out, out, jax.ShapeDtypeStruct((8, width), f32)],
        scratch_shapes=[pltpu.VMEM((rows, width), f32), pltpu.VMEM((rows, width), f32)],
        compiler_params=params(),
        name="attend_back",
    )(q, do_lo, do_hi, lse, k, v)


def pack_kernel(qkv_ref, out_ref, grad_ref, bias_ref, pack_ref):
    parts, rows, width = qkv_ref.shape
    for n in range(parts):
        pack_ref[n * rows : (n + 1) * rows, :] = qkv_ref[n]
    start = parts * rows
    for ref in (out_ref, grad_ref):
        for n in range(ref.shape[1] // width):
            pack_ref[start : start + width, :] = ref[:, n * width : (n + 1) * width]
            start += width
    pack_ref[start:, :] = bias_ref[...]


def pack(qkv, out, grad, bias):
    width = qkv.shape[2]
    rows = qkv.shape[0] * qkv.shape[1] + 2 * out.shape[1] + bias.shape[0]
    return pl.pallas_call(
        pack_kernel,
        out_shape=jax.ShapeDtypeStruct((rows, width), bf16),
        compiler_params=params(),
        name="pack",
    )(qkv, out, grad, bias)


def unpack_kernel(home_ref, mine_ref, got_ref, qkv_ref, both_ref, bias_ref):
    parts, rows, width = qkv_ref.shape
    first = home_ref[0] == 1
    pick = lambda start, size: jnp.where(
        first, mine_ref[start : start + size, :], got_ref[start : start + size, :]
    )
    for n in range(parts):
        qkv_ref[n] = pick(n * rows, rows)
    start = parts * rows
    for half in range(2):
        for n in range(both_ref.shape[2] // width):
            both_ref[half, :, n * width : (n + 1) * width] = pick(start, width)
            start += width
    bias_ref[...] = pick(start, bias_ref.shape[0])


def unpack(home, mine, got, parts, model, bias_rows):
    width = mine.shape[1]
    like = jax.ShapeDtypeStruct
    vmem = pl.BlockSpec(memory_space=pltpu.VMEM)
    return pl.pallas_call(
        unpack_kernel,
        in_specs=[pl.BlockSpec(memory_space=pltpu.SMEM), vmem, vmem],
        out_shape=[
            like((parts, model, width), bf16),
            like((2, width, model), bf16),
            like((bias_rows, width), bf16),
        ],
        compiler_params=params(),
        name="unpack",
    )(home, mine, got)


def middle_kernel(pieces_ref, w_ref, x_ref, bias_ref, scale_ref, gain_ref, shift_ref, sent_ref, a_ref, x1_ref):
    o = jnp.concatenate([pieces_ref[n] for n in range(pieces_ref.shape[0])], 1)
    w = jnp.concatenate([w_ref[n, 0] for n in range(w_ref.shape[0])], 0)
    a = dot_nn(o, w) + bias_ref[...]
    a_ref[...] = a
    x1 = x_ref[...].astype(f32) + scale_ref[...] * a
    x1_ref[...] = x1
    normed, _ = norm_pieces(x1)
    h = (normed * gain_ref[...] + shift_ref[...]).astype(bf16)
    for n in range(4):
        sent_ref[n] = h


def first_of_pairs(pairs):
    return pl.BlockSpec((pairs.shape[0], 1) + pairs.shape[2:], lambda i, *_: (0, 0, 0, 0))


def middle_rows(pieces, w, x, bias, scale, gain, shift):
    rows, model = x.shape
    like = jax.ShapeDtypeStruct
    return pl.pallas_call(
        middle_kernel,
        grid=(1,),
        in_specs=[whole(pieces.shape), first_of_pairs(w)]
        + [whole(v.shape) for v in (x, bias, scale, gain, shift)],
        out_specs=[whole((4, rows, model)), whole((rows, model)), whole((rows, model))],
        out_shape=[like((4, rows, model), bf16), like((rows, model), f32), like((rows, model), f32)],
        compiler_params=params(48),
        name="middle_rows",
    )(pieces, w, x, bias, scale, gain, shift)


def norm_back(upstream, normed, inv_dev, gain):
    scaled = upstream * gain
    return inv_dev * (
        scaled
        - jnp.mean(scaled, -1, keepdims=True)
        - normed * jnp.mean(scaled * normed, -1, keepdims=True)
    )


def norm_back_rows(upstream, values, gain):
    normed, inv_dev = norm_pieces(values)
    return normed, norm_back(upstream, normed, inv_dev, gain)


def middle_back_kernel(
    core_ref,
    got_ref,
    x1_ref,
    a_ref,
    gy_ref,
    gain_ref,
    scale_ref,
    bias_ref,
    w_ref,
    f_sum_ref,
    g1_ref,
    sent_ref,
    early_ref,
):
    total = lambda v: jnp.sum(v, 0, keepdims=True)
    dh2 = got_ref[0].astype(f32)
    for n in range(1, 4):
        dh2 = dh2 + got_ref[n].astype(f32)
    gy = gy_ref[0].astype(f32)
    normed, back = norm_back_rows(dh2, x1_ref[...], gain_ref[...])
    g1 = gy + back
    g1_ref[...] = g1
    da = (scale_ref[0:1, :] * g1).astype(bf16)
    w = jnp.concatenate([w_ref[n, 0] for n in range(w_ref.shape[0])], 0)
    do = dot_nt(da, w).astype(bf16)
    width = sent_ref.shape[2] - da.shape[1]
    first = core_ref[0] == 0
    half = da.shape[1] // 2
    piece = width // 2
    for n in range(4):
        low_part = do[:, n * piece : (n + 1) * piece]
        high_part = do[:, half + n * piece : half + (n + 1) * piece]
        sent_ref[n, :, : 2 * half] = da
        sent_ref[n, :, 2 * half : 2 * half + piece] = jnp.where(first, high_part, low_part)
        sent_ref[n, :, 2 * half + piece :] = jnp.where(first, low_part, high_part)
    early_ref[...] = jnp.zeros_like(early_ref)
    early_ref[2:3, :] = total(dh2 * normed)
    early_ref[3:4, :] = total(dh2)
    early_ref[4:5, :] = total(da.astype(f32))
    early_ref[5:6, :] = total((scale_ref[1:2, :] * gy).astype(bf16).astype(f32))
    early_ref[6:7, :] = total(g1 * a_ref[...])
    early_ref[7:8, :] = f_sum_ref[0:1, :] + bias_ref[...] * total(gy)


def middle_back(core, got, x1, a, gy, gain, scale, bias, w, f_sums, width):
    rows, model = x1.shape
    like = jax.ShapeDtypeStruct
    return pl.pallas_call(
        middle_back_kernel,
        grid_spec=pltpu.PrefetchScalarGridSpec(
            num_scalar_prefetch=1,
            grid=(1,),
            in_specs=[whole(v.shape) for v in (got, x1, a)]
            + [pl.BlockSpec((1,) + gy.shape[1:], lambda i, *_: (1, 0, 0))]
            + [whole(v.shape) for v in (gain, scale, bias)]
            + [first_of_pairs(w), whole(f_sums.shape)],
            out_specs=[
                whole((rows, model)),
                whole((4, rows, model + 2 * width)),
                whole((16, model)),
            ],
        ),
        out_shape=[
            like((rows, model), f32),
            like((4, rows, model + 2 * width), bf16),
            like((16, model), f32),
        ],
        compiler_params=params(48),
        name="middle_back",
    )(core, got, x1, a, gy, gain, scale, bias, w, f_sums)


def weight_kernel(h_ref, dq_ref, dk_ref, dv_ref, o_ref, da_lo_ref, da_hi_ref, out_ref, turned):
    @pl.when(pl.program_id(0) == 0)
    def _():
        for n, ref in enumerate((dq_ref, dk_ref, dv_ref, o_ref)):
            turned[n] = ref[...].T

    part = out_ref.shape[0] // 4
    for n in range(3):
        out_ref[n * part : (n + 1) * part, :] = dot_nn(turned[n], h_ref[...]).astype(bf16).T
    rows = da_lo_ref.shape[0]
    grad = dot_nn(turned[3, :, :rows], da_lo_ref[...]) + dot_nn(turned[3, :, rows:], da_hi_ref[...])
    width = out_ref.shape[1]
    for n in range(part // width):
        start = 3 * part + n * width
        out_ref[start : start + width, :] = grad[:, n * width : (n + 1) * width].astype(bf16)


def weight_grads(h, dq, dk, dv, o, da_lo, da_hi):
    rows, model = h.shape
    width = dq.shape[1]
    part = model // 4
    columns = lambda n: (0, n)
    return pl.pallas_call(
        weight_kernel,
        grid=(4,),
        in_specs=[pl.BlockSpec((rows, part), columns)]
        + [whole((rows, width))] * 4
        + [pl.BlockSpec((rows // 2, part), columns)] * 2,
        out_specs=pl.BlockSpec((4 * part, width), lambda n: (n, 0)),
        scratch_shapes=[pltpu.VMEM((4, width, rows), bf16)],
        out_shape=jax.ShapeDtypeStruct((16 * part, width), bf16),
        compiler_params=params(),
        name="weight_grads",
    )(h, dq, dk, dv, o, da_lo, da_hi)


def block_kernel(extra, here_ref, above_ref, below_ref, across_ref, out_ref):
    fine = here_ref.shape[0] - extra
    for n, ref in enumerate((here_ref, above_ref, across_ref, below_ref)):
        out_ref[n * fine : (n + 1) * fine, :] = ref[:fine, :]
    pair = lambda a, b: a[fine:, :].astype(f32) + b[fine:, :].astype(f32)
    total = pair(here_ref, across_ref) + pair(above_ref, below_ref)
    out_ref[4 * fine :, :] = total.astype(bf16)


def block_rows(extra, here, above, below, across):
    rows, width = here.shape
    return pl.pallas_call(
        functools.partial(block_kernel, extra),
        out_shape=jax.ShapeDtypeStruct((4 * (rows - extra) + extra, width), bf16),
        compiler_params=params(),
        name="block_rows",
    )(here, above, below, across)


def finish_kernel(place_ref, block_ref, other_ref, qkv_ref, out_ref):
    home = place_ref[0] == 1
    y = place_ref[1]
    parts, model, width = qkv_ref.shape
    part = model // 4
    fine = 2 * part
    for n in range(4):
        rows = slice(n * fine, (n + 1) * fine)
        mine, theirs = block_ref[rows, :].astype(f32), other_ref[rows, :].astype(f32)
        first, second = jnp.where(home, mine, theirs), jnp.where(home, theirs, mine)
        quarter = lax.rem(y + n, 4)
        at = pl.ds(pl.multiple_of(quarter * part, part), part)
        qkv_ref[0, at, :] = first[:part]
        qkv_ref[1, at, :] = first[part:]
        qkv_ref[2, at, :] = second[:part]
        for k in range(part // width):
            out_ref[quarter, :, k * width : (k + 1) * width] = second[
                part + k * width : part + (k + 1) * width
            ]


def finish(place, block, other, model):
    width = block.shape[1]
    like = jax.ShapeDtypeStruct
    vmem = pl.BlockSpec(memory_space=pltpu.VMEM)
    return pl.pallas_call(
        finish_kernel,
        in_specs=[pl.BlockSpec(memory_space=pltpu.SMEM), vmem, vmem],
        out_shape=[like((3, model, width), f32), like((4, width, model // 4), f32)],
        compiler_params=params(),
        name="finish",
    )(place, block, other)


def finish_hidden_kernel(home_ref, mine_ref, theirs_ref, one_ref, two_ref):
    home = home_ref[0] == 1
    half, width = mine_ref.shape[1:]
    model = one_ref.shape[0]
    for n in range(4):
        mine, theirs = mine_ref[n].astype(f32), theirs_ref[n].astype(f32)
        for k, rows in enumerate((jnp.where(home, mine, theirs), jnp.where(home, theirs, mine))):
            start = (2 * n + k) * half
            if start < model:
                one_ref[start : start + half, :] = rows
            else:
                column, row = divmod(start - model, width)
                two_ref[row : row + half, column * width : (column + 1) * width] = rows


def finish_hidden(home, mine, theirs, model):
    width = mine.shape[2]
    like = jax.ShapeDtypeStruct
    vmem = pl.BlockSpec(memory_space=pltpu.VMEM)
    return pl.pallas_call(
        finish_hidden_kernel,
        in_specs=[pl.BlockSpec(memory_space=pltpu.SMEM), vmem, vmem],
        out_shape=[like((model, width), f32), like((width, model), f32)],
        compiler_params=params(),
        name="finish_hidden",
    )(home, mine, theirs)


def join_kernel(lo_ref, f_lo_ref, got_ref, f_got_ref, out_ref):
    rows = out_ref.shape[1] // 2
    for n in range(4):
        block = slice(n * rows, (n + 1) * rows)
        for half, (one, two) in enumerate(((lo_ref, got_ref), (f_lo_ref, f_got_ref))):
            total = one[block, :].astype(f32) + two[block, :].astype(f32)
            out_ref[n, half * rows : (half + 1) * rows, :] = total.astype(bf16)


def join_rows(lo, f_lo, got, f_got):
    rows, model = lo.shape
    return pl.pallas_call(
        join_kernel,
        out_shape=jax.ShapeDtypeStruct((4, rows // 2, model), bf16),
        compiler_params=params(),
        name="join_rows",
    )(lo, f_lo, got, f_got)


def last_kernel(
    got_ref, x_ref, g1_ref, gain_ref, x1_ref, bias_ref, scale_ref, grad_ref, state_ref, sent_ref
):
    rows = x_ref.shape[0]
    total = got_ref[0].astype(f32)
    for n in range(1, 4):
        total = total + got_ref[n].astype(f32)
    _, back = norm_back_rows(total[:rows], x_ref[...].astype(f32), gain_ref[...])
    grad = g1_ref[...] + back
    state = x1_ref[...] + scale_ref[...] * (total[rows:] + bias_ref[...])
    grad_ref[...] = grad
    state_ref[...] = state
    sent_ref[:rows, :] = grad.astype(bf16)
    sent_ref[rows:, :] = state.astype(bf16)


def last_rows(got, x, g1, gain, x1, bias, scale):
    rows, model = x.shape
    like = jax.ShapeDtypeStruct
    return pl.pallas_call(
        last_kernel,
        out_shape=[
            like((rows, model), f32),
            like((rows, model), f32),
            like((2 * rows, model), bf16),
        ],
        compiler_params=params(),
        name="last_rows",
    )(got, x, g1, gain, x1, bias, scale)


def hidden_kernel(
    core_ref,
    h_lo_ref,
    h_hi_ref,
    g_ref,
    scale_ref,
    mine_ref,
    theirs_ref,
    b1_ref,
    h_ref,
    df_ref,
    m_ref,
    du_ref,
    lo_ref,
    hi_ref,
    f_lo_ref,
    f_hi_ref,
    du_sum_ref,
    f_sum_ref,
    w_ref,
):
    step = pl.program_id(0)
    model = h_lo_ref.shape[1]
    width = w_ref.shape[1]
    w1 = w_ref.at[:model]
    w2 = [w_ref.at[model + n : model + n + width] for n in range(0, model, width)]

    @pl.when(step == 0)
    def _():
        w_ref[...] = jnp.where(core_ref[1] == 1, mine_ref[...], theirs_ref[...])

    h = from_halves(h_lo_ref, h_hi_ref)
    h_ref[...] = h
    gy = jnp.concatenate([g_ref[n, 0] for n in range(g_ref.shape[0])], 0).astype(f32)
    df = (gy * scale_ref[...]).astype(bf16)
    df_ref[...] = df
    u = dot_nn(h, w1[...]) + b1_ref[...]
    phi = 0.5 * (1.0 + lax.erf(u * inv_root_two))
    m = (u * phi).astype(bf16)
    m_ref[...] = m
    dm = None
    for n, part in enumerate(w2):
        piece = dot_nt(df[:, n * width : (n + 1) * width], part[...])
        dm = piece if dm is None else dm + piece
    du = (dm * (phi + u * jnp.exp(-0.5 * u * u) * inv_root_two_pi)).astype(bf16)
    du_ref[...] = du
    to_halves(dot_nt(du, w1[...]).astype(bf16), lo_ref, hi_ref)
    f = jnp.concatenate([dot_nn(m, part[...]) for part in w2], 1)
    to_halves(f.astype(bf16), f_lo_ref, f_hi_ref)

    @pl.when(step == 0)
    def _():
        du_sum_ref[...] = jnp.zeros_like(du_sum_ref)
        f_sum_ref[...] = jnp.zeros_like(f_sum_ref)

    du_sum_ref[0:1, :] += jnp.sum(du.astype(f32), 0, keepdims=True)
    f_sum_ref[0:1, :] += jnp.sum(gy * f, 0, keepdims=True)


def hidden_block(core, h_lo, h_hi, g, scale, mine, theirs, b1):
    rows, model = 2 * h_lo.shape[0], h_lo.shape[1]
    width = mine.shape[1]
    blocks = rows // BLOCK
    each = BLOCK // g.shape[2]
    like = jax.ShapeDtypeStruct
    return pl.pallas_call(
        hidden_kernel,
        grid_spec=pltpu.PrefetchScalarGridSpec(
            num_scalar_prefetch=1,
            grid=(blocks,),
            in_specs=half_specs(model, blocks)
            + [
                pl.BlockSpec(
                    (each, 1) + g.shape[2:],
                    lambda i, core: ((i + core[0] * (blocks // 2)) % blocks, 1, 0, 0),
                ),
                whole((1, model)),
                whole(mine.shape),
                whole(mine.shape),
                whole((1, width)),
            ],
            out_specs=[
                rows_of(model),
                rows_in_order(model, blocks),
                rows_in_order(width, blocks),
                rows_of(width),
                whole((rows // 2, model)),
                whole((rows // 2, model)),
                whole((rows // 2, model)),
                whole((rows // 2, model)),
                whole((8, width)),
                whole((8, model)),
            ],
            scratch_shapes=[pltpu.VMEM(mine.shape, bf16)],
        ),
        out_shape=[
            like((rows, model), bf16),
            like((rows, model), bf16),
            like((rows, width), bf16),
            like((rows, width), bf16),
            like((rows // 2, model), bf16),
            like((rows // 2, model), bf16),
            like((rows // 2, model), bf16),
            like((rows // 2, model), bf16),
            like((8, width), f32),
            like((8, model), f32),
        ],
        compiler_params=params(40),
        name="hidden_block",
    )(core, h_lo, h_hi, g, scale, mine, theirs, b1)


def project_back_kernel(
    dq_ref, dk_ref, dv_ref, w_ref, x_lo_ref, x_hi_ref, early_ref, lo_ref, hi_ref, fold_ref, sum_ref
):
    step = pl.program_id(0)
    last = pl.num_programs(0) - 1
    dh = dot_nt(dq_ref[...], w_ref[0]) + dot_nt(dk_ref[...], w_ref[1]) + dot_nt(dv_ref[...], w_ref[2])
    normed, _ = norm_pieces(from_halves(x_lo_ref, x_hi_ref).astype(f32))

    @pl.when(step == 0)
    def _():
        sum_ref[...] = early_ref[...]

    to_halves(dh.astype(bf16), lo_ref, hi_ref)
    sum_ref[0:1, :] += jnp.sum(dh * normed, 0, keepdims=True)
    sum_ref[1:2, :] += jnp.sum(dh, 0, keepdims=True)

    @pl.when(step == last)
    def _():
        width = fold_ref.shape[1]
        for n in range(sum_ref.shape[1] // width):
            fold_ref[8 * n : 8 * n + 8, :] = sum_ref[0:8, n * width : (n + 1) * width]


def project_back(dq, dk, dv, w, x_lo, x_hi, early):
    rows, model = 2 * x_lo.shape[0], x_lo.shape[1]
    width = dq.shape[1]
    half = (rows // 2, model)
    folded = (8 * model // width, width)
    return pl.pallas_call(
        project_back_kernel,
        grid=(rows // BLOCK,),
        in_specs=[rows_of(width)] * 3
        + [whole(w.shape)]
        + half_specs(model, rows // BLOCK)
        + [whole((16, model))],
        out_specs=[whole(half), whole(half), whole(folded)],
        out_shape=[
            jax.ShapeDtypeStruct(half, bf16),
            jax.ShapeDtypeStruct(half, bf16),
            jax.ShapeDtypeStruct(folded, f32),
        ],
        scratch_shapes=[pltpu.VMEM((16, model), f32)],
        compiler_params=params(),
        name="project_back",
    )(dq, dk, dv, w, x_lo, x_hi, early)


AXES = ("dp", "tensor")


def members(key):
    found = {}
    for core in range(2):
        for z in range(4):
            for y in range(4):
                for xh in range(2):
                    for xl in range(2):
                        found.setdefault(key(xh, xl, y, z, core), []).append(
                            ((xl * 4 + y) * 2 + core) * 8 + xh * 4 + z
                        )
    return list(found.values())


def links(move):
    pairs = []
    for xh in range(2):
        for xl in range(2):
            for y in range(4):
                for z in range(4):
                    for core in range(2):
                        there = move(xh, xl, y, z, core)
                        if there is None:
                            continue
                        ph, pl_, py, pz, pc = there
                        pairs.append(
                            (
                                ((xl * 4 + y) * 2 + core) * 8 + xh * 4 + z,
                                ((pl_ * 4 + py % 4) * 2 + pc) * 8 + ph * 4 + pz % 4,
                            )
                        )
    return pairs


z_up = links(lambda xh, xl, y, z, c: (xh, xl, y, z + 1, c))
z_down = links(lambda xh, xl, y, z, c: (xh, xl, y, z - 1, c))
z_far = links(lambda xh, xl, y, z, c: (xh, xl, y, z + 2, c))
y_up = links(lambda xh, xl, y, z, c: (xh, xl, y + 1, z, c))
y_down = links(lambda xh, xl, y, z, c: (xh, xl, y - 1, z, c))
y_far = links(lambda xh, xl, y, z, c: (xh, xl, y + 2, z, c))
x_far = links(lambda xh, xl, y, z, c: (1 - xh, xl, y, z, c))
x_near = links(lambda xh, xl, y, z, c: (xh, 1 - xl, y, z, c))
cores = links(lambda xh, xl, y, z, c: (xh, xl, y, z, 1 - c))
regroup = links(lambda xh, xl, y, z, c: (c, xl, y, z, xh) if xh != c else None)
home = links(lambda xh, xl, y, z, c: (c, xl, y, z, c) if xh != c else None)
ring_z = members(lambda xh, xl, y, z, c: (xh, xl, y, c))
ring_y = members(lambda xh, xl, y, z, c: (xh, xl, z, c))
image = members(lambda xh, xl, y, z, c: (xh, xl, y))


def move(values, pairs):
    return lax.ppermute(values, AXES, pairs)


def exchange(values, groups):
    return lax.all_to_all(values, AXES, 0, 0, axis_index_groups=groups, tiled=True)


def gather(values, groups):
    return lax.all_gather(values, AXES, axis=0, axis_index_groups=groups, tiled=True)


def ring_from(values, up, down, far):
    return [values, move(values, down), move(values, up), move(values, far)]


def spread(rows):
    half = exchange(jnp.concatenate([rows] * 4, 0), ring_z)
    return half, move(half, cores)


def terms(values):
    first = lax.reduce_precision(values, 8, 7)
    rest = values - first
    second = lax.reduce_precision(rest, 8, 7)
    return low(jnp.concatenate([first, second, rest - second], 0))


def after(values, *others):
    return lax.optimization_barrier((values, *others))[0]


def wide(values):
    return values.astype(f32)


def low(values):
    return values.astype(bf16)


def turn(values, axis, start):
    return lax.dynamic_slice_in_dim(jnp.concatenate([values, values], axis), start % 4, 4, axis)


def unfold(values, rows):
    return jnp.concatenate([values[n : n + rows] for n in range(0, values.shape[0], rows)], 1)


def at_home(here, there, home_here):
    return jnp.where(home_here, here, there), jnp.where(home_here, there, here)


def shards(
    tokens,
    cotangent,
    w_qkv,
    qv_bias,
    w_out,
    w_fc1,
    b_fc1,
    w_fc2,
    norm_gain,
    norm_shift,
    out_bias,
    layer_scale,
):
    layer = 0
    place = lax.axis_index("dp")
    core = place % 2
    y = (place // 2) % 4
    x_hi = lax.axis_index("tensor") // 4
    z = lax.axis_index("tensor") % 4
    home_here = x_hi == core
    core_arg = core.astype(jnp.int32).reshape(1)
    home_arg = home_here.astype(jnp.int32).reshape(1)
    width = w_qkv.shape[3]
    hidden_here = w_fc1.shape[2]
    own, model = tokens.shape

    def regrouped(values):
        return jnp.where(home_here, values, move(values, regroup))

    rows_in = regrouped(tokens)
    bias_terms = terms(jnp.concatenate([qv_bias[layer].reshape(-1, width), b_fc1.reshape(-1, width)], 0))
    bias_rows = bias_terms.shape[0]
    bias_terms = jnp.pad(bias_terms, ((0, -bias_rows % 16), (0, 0)))
    first = pack(jnp.moveaxis(w_qkv[layer], 1, 0), w_out[layer], cotangent, bias_terms)
    first_got = move(after(first, rows_in), regroup)
    tokens_lo = exchange(jnp.concatenate([rows_in] * 4, 0), ring_z)
    fc_mine = jnp.concatenate(
        [w_fc1[layer], w_fc2[layer][:, :hidden_here], w_fc2[layer][:, hidden_here:]], 0
    )
    first_got, tokens_lo, fc_mine = lax.optimization_barrier((first_got, tokens_lo, fc_mine))
    tokens_hi = move(tokens_lo, cores)
    qkv_in, out_grad, biases = unpack(
        home_arg, first, first_got, 3, model, bias_terms.shape[0]
    )
    biases = jnp.sum(wide(biases[:bias_rows]).reshape(3, -1, width), 0)
    qv_in = biases[:2]
    hidden_bias = biases[2:].reshape(1, hidden_here)
    out_grad_full = gather(out_grad.reshape(2 * own, model), image).reshape(8, 2, own, model)

    normed_full, query_rows, key_rows, value_rows = project(
        tokens_lo, tokens_hi, norm_gain[layer, 0:1], norm_shift[layer, 0:1], qkv_in, qv_in
    )
    mixed, mixed_own, log_total = attend(core_arg, query_rows, key_rows, value_rows)
    pieces = exchange(mixed, image).reshape(8, own, width)
    fc_got = move(after(fc_mine, pieces), regroup)
    sent_two, branch, middle = middle_rows(
        pieces,
        out_grad_full,
        rows_in,
        out_bias[layer, 0:1],
        layer_scale[layer, 0:1],
        norm_gain[layer, 1:2],
        norm_shift[layer, 1:2],
    )
    two_lo = exchange(sent_two, ring_z).reshape(4 * own, model)
    two_hi = move(two_lo, cores)
    half = two_lo.shape[0]

    normed_two_full, down_full, hidden, act_grad, lo_two, hi_two, f_lo, f_hi, du_sums, f_sums = (
        hidden_block(
            jnp.concatenate([core_arg, home_arg]),
            two_lo,
            two_hi,
            out_grad_full,
            layer_scale[layer, 1:2],
            fc_mine,
            fc_got,
            hidden_bias,
        )
    )
    mine_two = low(wide(lo_two) + wide(move(hi_two, cores)))
    got_two = exchange(mine_two.reshape(4, own, model), ring_z)
    grad_b1 = du_sums[0]

    grad_fc2 = jnp.einsum("gf,gd->fd", hidden, down_full, preferred_element_type=f32)
    grad_fc1 = jnp.einsum("gd,gf->df", normed_two_full, act_grad, preferred_element_type=f32)
    joined = jnp.concatenate(
        [low(grad_fc1), low(grad_fc2[:, : model // 2]), low(grad_fc2[:, model // 2 :])], 0
    )
    joined, got_two = lax.optimization_barrier((joined, got_two))
    fc_quarter_y = lax.psum_scatter(
        joined, AXES, scatter_dimension=0, axis_index_groups=ring_y, tiled=True
    )
    gradient_two, sent, early = middle_back(
        core_arg,
        got_two,
        middle,
        branch,
        out_grad,
        norm_gain[layer, 1:2],
        layer_scale[layer],
        out_bias[layer, 1:2],
        out_grad_full,
        f_sums,
        width,
    )
    back_lo = exchange(sent, ring_z).reshape(4 * own, model + 2 * width)
    back_hi = move(back_lo[:, : model + width], cores)
    query_grad, key_grad, value_grad, qv_sums = attend_back(
        query_rows,
        key_rows,
        value_rows,
        back_lo,
        (model + width) // width,
        back_hi,
        model // width,
        log_total,
    )
    fc_quarter = low(wide(fc_quarter_y) + wide(move(fc_quarter_y, x_near)))
    query_grad, fc_quarter = lax.optimization_barrier((query_grad, fc_quarter))
    payload = weight_grads(
        normed_full, query_grad, key_grad, value_grad, mixed_own, back_lo, back_hi
    )
    query_grad = after(query_grad, payload)
    fc_quarter = low(wide(fc_quarter) + wide(move(fc_quarter, x_far)))
    lo, hi, small = project_back(
        query_grad, key_grad, value_grad, qkv_in, tokens_lo, tokens_hi, early
    )
    got = exchange(join_rows(lo, f_lo, move(hi, cores), move(f_hi, cores)), ring_z)

    quarter = payload.shape[0] // 4
    got_q = exchange(payload, ring_y)
    got_q, fc_quarter = lax.optimization_barrier((got_q, fc_quarter))
    rows_q = jnp.sum(wide(got_q).reshape(4, quarter, width), 0)
    wide_bias = jnp.concatenate(
        [qv_sums[:2].reshape(-1), grad_b1, jnp.zeros((model - 2 * width - hidden_here,), f32)]
    )
    wide_bias = jnp.concatenate([wide_bias, jnp.zeros_like(wide_bias)]).reshape(-1, width)
    flow = jnp.concatenate([low(rows_q), low(small), low(wide_bias)], 0)
    flow = low(wide(flow) + wide(move(flow, x_far)))
    fc_half = fc_quarter.shape[0] // 2
    fc_part = jnp.where(home_here, fc_quarter[:fc_half], move(fc_quarter[fc_half:], cores))
    flow = low(wide(flow) + wide(move(flow, x_near)))
    flow, fc_part = lax.optimization_barrier((flow, fc_part))
    fc_all = gather(fc_part, ring_y).reshape(4, fc_half, -1)
    fine = quarter // 2
    kept = jnp.where(home_here, flow[:fine], move(flow[fine:quarter], cores))
    sent_y = jnp.concatenate([kept, flow[quarter:]], 0)
    got_y = ring_from(sent_y, y_up, y_down, y_far)
    (here, above, below, across), got = lax.optimization_barrier((tuple(got_y), got))
    gradient_one, state_one, rows_sent = last_rows(
        got,
        rows_in,
        gradient_two,
        norm_gain[layer, 0:1],
        middle,
        out_bias[layer, 1:2],
        layer_scale[layer, 1:2],
    )
    rows_back = wide(move(rows_sent, regroup))
    gradient_out = jnp.where(home_here, gradient_one, rows_back[:own])
    state_out = jnp.where(home_here, state_one, rows_back[own:])
    extra = flow.shape[0] - quarter
    block = block_rows(extra, here, above, below, across)
    tail = block[4 * fine :]
    other = move(block, cores)
    small_rows = small.shape[0]
    small = low(wide(tail[:small_rows]) + wide(other[4 * fine : 4 * fine + small_rows]))
    small = jnp.sum(wide(exchange(jnp.concatenate([small] * 4, 0), ring_z)).reshape(4, -1, width), 0)
    small_total = unfold(small, 8)
    total_qkv, total_out = finish(
        jnp.concatenate([home_arg, y.astype(jnp.int32).reshape(1)]), block, other, model
    )
    total_qkv = jnp.moveaxis(total_qkv, 0, 1)
    total_out = jnp.moveaxis(total_out, 0, 1).reshape(width, model)
    total_fc1, total_fc2 = finish_hidden(home_arg, fc_all, move(fc_all, cores), model)
    bias_rows_mine = jnp.where(home_here, tail[small_rows:], other[4 * fine + small_rows :])
    bias_total = wide(bias_rows_mine).reshape(2, model)[:1]
    return (
        state_out,
        gradient_out,
        total_qkv[None],
        bias_total[:, : 2 * width].reshape(1, 2, width),
        total_out[None],
        total_fc1[None],
        bias_total[:, 2 * width : 2 * width + hidden_here],
        total_fc2[None],
        jnp.stack([small_total[0], small_total[2]])[None],
        jnp.stack([small_total[1], small_total[3]])[None],
        small_total[4:6][None],
        small_total[6:8][None],
    )


def solution(mesh):
    return jax.shard_map(
        shards,
        mesh=mesh,
        in_specs=(
            P(("dp", "tensor"), None),
            P(("dp", "tensor"), None),
            P(None, None, None, "tensor"),
            P(None, None, "tensor"),
            P(None, "tensor", None),
            P(None, None, "tensor"),
            P(None, "tensor"),
            P(None, "tensor", None),
            P(),
            P(),
            P(),
            P(),
        ),
        out_specs=(
            P(("dp", "tensor"), None),
            P(("dp", "tensor"), None),
            P(None, None, None, "tensor"),
            P(None, None, "tensor"),
            P(None, "tensor", None),
            P(None, None, "tensor"),
            P(None, "tensor"),
            P(None, "tensor", None),
            P(),
            P(),
            P(),
            P(),
        ),
        check_vma=False,
    )
```

```python
import functools

import jax
import jax.numpy as jnp
from jax import lax
from jax.experimental import pallas as pl
from jax.experimental.pallas import tpu as pltpu
from jax.sharding import PartitionSpec as P

HD = 64
BLOCK = 256
inv_root_two = 0.7071067811865476
inv_root_two_pi = 0.3989422804014327
f32 = jnp.float32
bf16 = jnp.bfloat16


def dot_nn(a, b):
    return lax.dot_general(a, b, (((1,), (0,)), ((), ())), preferred_element_type=f32)


def dot_nt(a, b):
    return lax.dot_general(a, b, (((1,), (1,)), ((), ())), preferred_element_type=f32)


def params(mebibytes=24):
    return pltpu.CompilerParams(vmem_limit_bytes=mebibytes * 1024 * 1024)


def whole(shape):
    return pl.BlockSpec(shape, lambda i, *_: (0,) * len(shape))


def rows_of(width, block=BLOCK):
    return pl.BlockSpec((block, width), lambda i, *_: (i, 0))


def rows_in_order(width, blocks):
    return pl.BlockSpec((BLOCK, width), lambda i, core: ((i + core[0] * (blocks // 2)) % blocks, 0))


def half_specs(width, blocks):
    half = blocks // 2
    return [
        pl.BlockSpec((BLOCK, width), lambda i, *_: (jnp.minimum(i, half - 1), 0)),
        pl.BlockSpec((BLOCK, width), lambda i, *_: (jnp.maximum(i - half, 0), 0)),
    ]


def from_halves(lo_ref, hi_ref):
    return jnp.where(pl.program_id(0) < pl.num_programs(0) // 2, lo_ref[...], hi_ref[...])


def to_halves(values, lo_ref, hi_ref):
    step = pl.program_id(0)
    half = pl.num_programs(0) // 2

    @pl.when(step < half)
    def _():
        lo_ref[pl.ds(pl.multiple_of(step * BLOCK, BLOCK), BLOCK), :] = values

    @pl.when(step >= half)
    def _():
        hi_ref[pl.ds(pl.multiple_of((step - half) * BLOCK, BLOCK), BLOCK), :] = values


def norm_pieces(values):
    centred = values - jnp.mean(values, -1, keepdims=True)
    inv_dev = lax.rsqrt(jnp.mean(centred * centred, -1, keepdims=True) + 1e-06)
    return centred * inv_dev, inv_dev


def project_kernel(lo_ref, hi_ref, gain_ref, shift_ref, w_ref, bias_ref, h_ref, q_ref, k_ref, v_ref):
    normed, _ = norm_pieces(from_halves(lo_ref, hi_ref).astype(f32))
    h = (normed * gain_ref[...] + shift_ref[...]).astype(bf16)
    h_ref[...] = h
    q_ref[...] = (dot_nn(h, w_ref[0]) + bias_ref[0:1, :]).astype(bf16)
    k_ref[...] = dot_nn(h, w_ref[1]).astype(bf16)
    v_ref[...] = (dot_nn(h, w_ref[2]) + bias_ref[1:2, :]).astype(bf16)


def project(lo, hi, gain, shift, w, bias):
    rows, model = 2 * lo.shape[0], lo.shape[1]
    width = w.shape[2]
    out = jax.ShapeDtypeStruct((rows, width), bf16)
    return pl.pallas_call(
        project_kernel,
        grid=(rows // BLOCK,),
        in_specs=half_specs(model, rows // BLOCK)
        + [whole((1, model)), whole((1, model)), whole(w.shape), whole(bias.shape)],
        out_specs=[rows_of(model)] + [rows_of(width)] * 3,
        out_shape=[jax.ShapeDtypeStruct((rows, model), bf16), out, out, out],
        compiler_params=params(),
        name="norm_project",
    )(lo, hi, gain, shift, w, bias)


def lane_mask(shape, head, dim):
    return (lax.broadcasted_iota(jnp.int32, shape, dim) // HD) == head


def only_head(values, head, dim=1):
    return jnp.where(lane_mask(values.shape, head, dim), values, jnp.zeros_like(values))


def attend_kernel(core_ref, q_ref, k_ref, v_ref, o_ref, own_ref, lse_ref):
    q = q_ref[...] * jnp.asarray(HD**-0.5, bf16)
    v_t = v_ref[...].T
    total = None
    for head in range(q.shape[1] // HD):
        scores = dot_nt(k_ref[...], only_head(q, head))
        top = jnp.max(scores, 0, keepdims=True)
        shifted = jnp.exp(scores - top)
        row_sum = jnp.sum(shifted, 0, keepdims=True)
        prob = (shifted * (1.0 / row_sum)).astype(bf16)
        lse_ref[head : head + 1, :] = top + jnp.log(row_sum)
        piece = dot_nn(only_head(v_t, head, 0), prob)
        total = piece if total is None else total + piece
    o = total.astype(bf16).T
    o_ref[...] = o
    own_ref[...] = o


def attend(core, q, k, v):
    rows, width = q.shape
    heads = width // HD
    return pl.pallas_call(
        attend_kernel,
        grid_spec=pltpu.PrefetchScalarGridSpec(
            num_scalar_prefetch=1,
            grid=(rows // BLOCK,),
            in_specs=[rows_of(width), whole(k.shape), whole(v.shape)],
            out_specs=[
                rows_in_order(width, rows // BLOCK),
                rows_of(width),
                pl.BlockSpec((heads, BLOCK), lambda i, *_: (0, i)),
            ],
        ),
        out_shape=[jax.ShapeDtypeStruct((rows, width), bf16)] * 2 + [jax.ShapeDtypeStruct((heads, rows), f32)],
        compiler_params=params(),
        name="attend",
    )(core, q, k, v)


def attend_back_kernel(
    q_ref,
    do_lo_ref,
    do_hi_ref,
    lse_ref,
    k_ref,
    v_ref,
    dq_ref,
    dk_ref,
    dv_ref,
    sum_ref,
    dk_acc,
    dv_acc,
):
    step = pl.program_id(0)
    last = pl.num_programs(0) - 1
    scale = HD**-0.5

    @pl.when(step == 0)
    def _():
        dk_acc[...] = jnp.zeros_like(dk_acc)
        dv_acc[...] = jnp.zeros_like(dv_acc)
        sum_ref[...] = jnp.zeros_like(sum_ref)

    q = q_ref[...] * jnp.asarray(scale, bf16)
    do = from_halves(do_lo_ref, do_hi_ref)
    k_t = k_ref[...].T
    dq_t = None
    for head in range(q.shape[1] // HD):
        q_h = only_head(q, head)
        do_h = only_head(do, head)
        prob = jnp.exp(dot_nt(k_ref[...], q_h) - lse_ref[head : head + 1, :])
        d_prob = dot_nt(v_ref[...], do_h)
        row = jnp.sum(d_prob * prob, 0, keepdims=True)
        d_score = (prob * (d_prob - row)).astype(bf16)
        dv_acc[...] += dot_nn(prob.astype(bf16), do_h)
        dk_acc[...] += dot_nn(d_score, q_h)
        piece = dot_nn(only_head(k_t, head, 0), d_score)
        dq_t = piece if dq_t is None else dq_t + piece
    dq = (dq_t * scale).astype(bf16).T
    dq_ref[...] = dq
    sum_ref[0:1, :] += jnp.sum(dq.astype(f32), 0, keepdims=True)

    @pl.when(step == last)
    def _():
        dk_ref[...] = dk_acc[...].astype(bf16)
        dv = dv_acc[...].astype(bf16)
        dv_ref[...] = dv
        sum_ref[1:2, :] = jnp.sum(dv.astype(f32), 0, keepdims=True)


def attend_back(q, k, v, do_lo, lo_block, do_hi, hi_block, lse):
    rows, width = q.shape
    heads = width // HD
    half = rows // BLOCK // 2
    out = jax.ShapeDtypeStruct((rows, width), bf16)
    return pl.pallas_call(
        attend_back_kernel,
        grid=(rows // BLOCK,),
        in_specs=[
            rows_of(width),
            pl.BlockSpec((BLOCK, width), lambda i: (jnp.minimum(i, half - 1), lo_block)),
            pl.BlockSpec((BLOCK, width), lambda i: (jnp.maximum(i - half, 0), hi_block)),
            pl.BlockSpec((heads, BLOCK), lambda i: (0, i)),
            whole(k.shape),
            whole(v.shape),
        ],
        out_specs=[rows_of(width), whole(k.shape), whole(v.shape), whole((8, width))],
        out_shape=[out, out, out, jax.ShapeDtypeStruct((8, width), f32)],
        scratch_shapes=[pltpu.VMEM((rows, width), f32), pltpu.VMEM((rows, width), f32)],
        compiler_params=params(),
        name="attend_back",
    )(q, do_lo, do_hi, lse, k, v)


def pack_kernel(qkv_ref, out_ref, grad_ref, bias_ref, pack_ref):
    parts, rows, width = qkv_ref.shape
    for n in range(parts):
        pack_ref[n * rows : (n + 1) * rows, :] = qkv_ref[n]
    start = parts * rows
    for ref in (out_ref, grad_ref):
        for n in range(ref.shape[1] // width):
            pack_ref[start : start + width, :] = ref[:, n * width : (n + 1) * width]
            start += width
    pack_ref[start:, :] = bias_ref[...]


def pack(qkv, out, grad, bias):
    width = qkv.shape[2]
    rows = qkv.shape[0] * qkv.shape[1] + 2 * out.shape[1] + bias.shape[0]
    return pl.pallas_call(
        pack_kernel,
        out_shape=jax.ShapeDtypeStruct((rows, width), bf16),
        compiler_params=params(),
        name="pack",
    )(qkv, out, grad, bias)


def unpack_kernel(home_ref, mine_ref, got_ref, qkv_ref, both_ref, bias_ref):
    parts, rows, width = qkv_ref.shape
    first = home_ref[0] == 1
    pick = lambda start, size: jnp.where(
        first, mine_ref[start : start + size, :], got_ref[start : start + size, :]
    )
    for n in range(parts):
        qkv_ref[n] = pick(n * rows, rows)
    start = parts * rows
    for half in range(2):
        for n in range(both_ref.shape[2] // width):
            both_ref[half, :, n * width : (n + 1) * width] = pick(start, width)
            start += width
    bias_ref[...] = pick(start, bias_ref.shape[0])


def unpack(home, mine, got, parts, model, bias_rows):
    width = mine.shape[1]
    like = jax.ShapeDtypeStruct
    vmem = pl.BlockSpec(memory_space=pltpu.VMEM)
    return pl.pallas_call(
        unpack_kernel,
        in_specs=[pl.BlockSpec(memory_space=pltpu.SMEM), vmem, vmem],
        out_shape=[
            like((parts, model, width), bf16),
            like((2, width, model), bf16),
            like((bias_rows, width), bf16),
        ],
        compiler_params=params(),
        name="unpack",
    )(home, mine, got)


def middle_kernel(pieces_ref, w_ref, x_ref, bias_ref, scale_ref, gain_ref, shift_ref, sent_ref, a_ref, x1_ref):
    o = jnp.concatenate([pieces_ref[n] for n in range(pieces_ref.shape[0])], 1)
    w = jnp.concatenate([w_ref[n, 0] for n in range(w_ref.shape[0])], 0)
    a = dot_nn(o, w) + bias_ref[...]
    a_ref[...] = a
    x1 = x_ref[...].astype(f32) + scale_ref[...] * a
    x1_ref[...] = x1
    normed, _ = norm_pieces(x1)
    h = (normed * gain_ref[...] + shift_ref[...]).astype(bf16)
    for n in range(4):
        sent_ref[n] = h


def first_of_pairs(pairs):
    return pl.BlockSpec((pairs.shape[0], 1) + pairs.shape[2:], lambda i, *_: (0, 0, 0, 0))


def middle_rows(pieces, w, x, bias, scale, gain, shift):
    rows, model = x.shape
    like = jax.ShapeDtypeStruct
    return pl.pallas_call(
        middle_kernel,
        grid=(1,),
        in_specs=[whole(pieces.shape), first_of_pairs(w)]
        + [whole(v.shape) for v in (x, bias, scale, gain, shift)],
        out_specs=[whole((4, rows, model)), whole((rows, model)), whole((rows, model))],
        out_shape=[like((4, rows, model), bf16), like((rows, model), f32), like((rows, model), f32)],
        compiler_params=params(48),
        name="middle_rows",
    )(pieces, w, x, bias, scale, gain, shift)


def norm_back(upstream, normed, inv_dev, gain):
    scaled = upstream * gain
    return inv_dev * (
        scaled
        - jnp.mean(scaled, -1, keepdims=True)
        - normed * jnp.mean(scaled * normed, -1, keepdims=True)
    )


def norm_back_rows(upstream, values, gain):
    normed, inv_dev = norm_pieces(values)
    return normed, norm_back(upstream, normed, inv_dev, gain)


def middle_back_kernel(
    core_ref,
    got_ref,
    x1_ref,
    a_ref,
    gy_ref,
    gain_ref,
    scale_ref,
    bias_ref,
    w_ref,
    f_sum_ref,
    g1_ref,
    sent_ref,
    early_ref,
):
    total = lambda v: jnp.sum(v, 0, keepdims=True)
    dh2 = got_ref[0].astype(f32)
    for n in range(1, 4):
        dh2 = dh2 + got_ref[n].astype(f32)
    gy = gy_ref[0].astype(f32)
    normed, back = norm_back_rows(dh2, x1_ref[...], gain_ref[...])
    g1 = gy + back
    g1_ref[...] = g1
    da = (scale_ref[0:1, :] * g1).astype(bf16)
    w = jnp.concatenate([w_ref[n, 0] for n in range(w_ref.shape[0])], 0)
    do = dot_nt(da, w).astype(bf16)
    width = sent_ref.shape[2] - da.shape[1]
    first = core_ref[0] == 0
    half = da.shape[1] // 2
    piece = width // 2
    for n in range(4):
        low_part = do[:, n * piece : (n + 1) * piece]
        high_part = do[:, half + n * piece : half + (n + 1) * piece]
        sent_ref[n, :, : 2 * half] = da
        sent_ref[n, :, 2 * half : 2 * half + piece] = jnp.where(first, high_part, low_part)
        sent_ref[n, :, 2 * half + piece :] = jnp.where(first, low_part, high_part)
    early_ref[...] = jnp.zeros_like(early_ref)
    early_ref[2:3, :] = total(dh2 * normed)
    early_ref[3:4, :] = total(dh2)
    early_ref[4:5, :] = total(da.astype(f32))
    early_ref[5:6, :] = total((scale_ref[1:2, :] * gy).astype(bf16).astype(f32))
    early_ref[6:7, :] = total(g1 * a_ref[...])
    early_ref[7:8, :] = f_sum_ref[0:1, :] + bias_ref[...] * total(gy)


def middle_back(core, got, x1, a, gy, gain, scale, bias, w, f_sums, width):
    rows, model = x1.shape
    like = jax.ShapeDtypeStruct
    return pl.pallas_call(
        middle_back_kernel,
        grid_spec=pltpu.PrefetchScalarGridSpec(
            num_scalar_prefetch=1,
            grid=(1,),
            in_specs=[whole(v.shape) for v in (got, x1, a)]
            + [pl.BlockSpec((1,) + gy.shape[1:], lambda i, *_: (1, 0, 0))]
            + [whole(v.shape) for v in (gain, scale, bias)]
            + [first_of_pairs(w), whole(f_sums.shape)],
            out_specs=[
                whole((rows, model)),
                whole((4, rows, model + 2 * width)),
                whole((16, model)),
            ],
        ),
        out_shape=[
            like((rows, model), f32),
            like((4, rows, model + 2 * width), bf16),
            like((16, model), f32),
        ],
        compiler_params=params(48),
        name="middle_back",
    )(core, got, x1, a, gy, gain, scale, bias, w, f_sums)


def weight_kernel(h_ref, dq_ref, dk_ref, dv_ref, o_ref, da_lo_ref, da_hi_ref, out_ref, turned):
    @pl.when(pl.program_id(0) == 0)
    def _():
        for n, ref in enumerate((dq_ref, dk_ref, dv_ref, o_ref)):
            turned[n] = ref[...].T

    part = out_ref.shape[0] // 4
    for n in range(3):
        out_ref[n * part : (n + 1) * part, :] = dot_nn(turned[n], h_ref[...]).astype(bf16).T
    rows = da_lo_ref.shape[0]
    grad = dot_nn(turned[3, :, :rows], da_lo_ref[...]) + dot_nn(turned[3, :, rows:], da_hi_ref[...])
    width = out_ref.shape[1]
    for n in range(part // width):
        start = 3 * part + n * width
        out_ref[start : start + width, :] = grad[:, n * width : (n + 1) * width].astype(bf16)


def weight_grads(h, dq, dk, dv, o, da_lo, da_hi):
    rows, model = h.shape
    width = dq.shape[1]
    part = model // 4
    columns = lambda n: (0, n)
    return pl.pallas_call(
        weight_kernel,
        grid=(4,),
        in_specs=[pl.BlockSpec((rows, part), columns)]
        + [whole((rows, width))] * 4
        + [pl.BlockSpec((rows // 2, part), columns)] * 2,
        out_specs=pl.BlockSpec((4 * part, width), lambda n: (n, 0)),
        scratch_shapes=[pltpu.VMEM((4, width, rows), bf16)],
        out_shape=jax.ShapeDtypeStruct((16 * part, width), bf16),
        compiler_params=params(),
        name="weight_grads",
    )(h, dq, dk, dv, o, da_lo, da_hi)


def block_kernel(extra, here_ref, above_ref, below_ref, across_ref, out_ref):
    fine = here_ref.shape[0] - extra
    for n, ref in enumerate((here_ref, above_ref, across_ref, below_ref)):
        out_ref[n * fine : (n + 1) * fine, :] = ref[:fine, :]
    pair = lambda a, b: a[fine:, :].astype(f32) + b[fine:, :].astype(f32)
    total = pair(here_ref, across_ref) + pair(above_ref, below_ref)
    out_ref[4 * fine :, :] = total.astype(bf16)


def block_rows(extra, here, above, below, across):
    rows, width = here.shape
    return pl.pallas_call(
        functools.partial(block_kernel, extra),
        out_shape=jax.ShapeDtypeStruct((4 * (rows - extra) + extra, width), bf16),
        compiler_params=params(),
        name="block_rows",
    )(here, above, below, across)


def finish_kernel(place_ref, block_ref, other_ref, qkv_ref, out_ref):
    home = place_ref[0] == 1
    y = place_ref[1]
    parts, model, width = qkv_ref.shape
    part = model // 4
    fine = 2 * part
    for n in range(4):
        rows = slice(n * fine, (n + 1) * fine)
        mine, theirs = block_ref[rows, :].astype(f32), other_ref[rows, :].astype(f32)
        first, second = jnp.where(home, mine, theirs), jnp.where(home, theirs, mine)
        quarter = lax.rem(y + n, 4)
        at = pl.ds(pl.multiple_of(quarter * part, part), part)
        qkv_ref[0, at, :] = first[:part]
        qkv_ref[1, at, :] = first[part:]
        qkv_ref[2, at, :] = second[:part]
        for k in range(part // width):
            column = pl.multiple_of(quarter * part + k * width, width)
            out_ref[:, pl.ds(column, width)] = second[part + k * width : part + (k + 1) * width]


def finish(place, block, other, model):
    width = block.shape[1]
    like = jax.ShapeDtypeStruct
    vmem = pl.BlockSpec(memory_space=pltpu.VMEM)
    return pl.pallas_call(
        finish_kernel,
        in_specs=[pl.BlockSpec(memory_space=pltpu.SMEM), vmem, vmem],
        out_shape=[like((3, model, width), f32), like((width, model), f32)],
        compiler_params=params(),
        name="finish",
    )(place, block, other)


def finish_hidden_kernel(home_ref, mine_ref, theirs_ref, one_ref, two_ref):
    home = home_ref[0] == 1
    half, width = mine_ref.shape[1:]
    model = one_ref.shape[0]
    for n in range(4):
        mine, theirs = mine_ref[n].astype(f32), theirs_ref[n].astype(f32)
        for k, rows in enumerate((jnp.where(home, mine, theirs), jnp.where(home, theirs, mine))):
            start = (2 * n + k) * half
            if start < model:
                one_ref[start : start + half, :] = rows
            else:
                column, row = divmod(start - model, width)
                two_ref[row : row + half, column * width : (column + 1) * width] = rows


def finish_hidden(home, mine, theirs, model):
    width = mine.shape[2]
    like = jax.ShapeDtypeStruct
    vmem = pl.BlockSpec(memory_space=pltpu.VMEM)
    return pl.pallas_call(
        finish_hidden_kernel,
        in_specs=[pl.BlockSpec(memory_space=pltpu.SMEM), vmem, vmem],
        out_shape=[like((model, width), f32), like((width, model), f32)],
        compiler_params=params(),
        name="finish_hidden",
    )(home, mine, theirs)


def join_kernel(lo_ref, f_lo_ref, got_ref, f_got_ref, out_ref):
    rows = out_ref.shape[1] // 2
    for n in range(4):
        block = slice(n * rows, (n + 1) * rows)
        for half, (one, two) in enumerate(((lo_ref, got_ref), (f_lo_ref, f_got_ref))):
            total = one[block, :].astype(f32) + two[block, :].astype(f32)
            out_ref[n, half * rows : (half + 1) * rows, :] = total.astype(bf16)


def join_rows(lo, f_lo, got, f_got):
    rows, model = lo.shape
    return pl.pallas_call(
        join_kernel,
        out_shape=jax.ShapeDtypeStruct((4, rows // 2, model), bf16),
        compiler_params=params(),
        name="join_rows",
    )(lo, f_lo, got, f_got)


def last_kernel(
    got_ref, x_ref, g1_ref, gain_ref, x1_ref, bias_ref, scale_ref, grad_ref, state_ref, sent_ref
):
    rows = x_ref.shape[0]
    total = got_ref[0].astype(f32)
    for n in range(1, 4):
        total = total + got_ref[n].astype(f32)
    _, back = norm_back_rows(total[:rows], x_ref[...].astype(f32), gain_ref[...])
    grad = g1_ref[...] + back
    state = x1_ref[...] + scale_ref[...] * (total[rows:] + bias_ref[...])
    grad_ref[...] = grad
    state_ref[...] = state
    sent_ref[:rows, :] = grad.astype(bf16)
    sent_ref[rows:, :] = state.astype(bf16)


def last_rows(got, x, g1, gain, x1, bias, scale):
    rows, model = x.shape
    like = jax.ShapeDtypeStruct
    return pl.pallas_call(
        last_kernel,
        out_shape=[
            like((rows, model), f32),
            like((rows, model), f32),
            like((2 * rows, model), bf16),
        ],
        compiler_params=params(),
        name="last_rows",
    )(got, x, g1, gain, x1, bias, scale)


def settle_kernel(home_ref, grad_ref, state_ref, back_ref, grad_out_ref, state_out_ref):
    home = home_ref[0] == 1
    rows = grad_ref.shape[0]
    grad_out_ref[...] = jnp.where(home, grad_ref[...], back_ref[:rows, :].astype(f32))
    state_out_ref[...] = jnp.where(home, state_ref[...], back_ref[rows:, :].astype(f32))


def settle(home, grad, state, back):
    vmem = pl.BlockSpec(memory_space=pltpu.VMEM)
    return pl.pallas_call(
        settle_kernel,
        in_specs=[pl.BlockSpec(memory_space=pltpu.SMEM)] + [vmem] * 3,
        out_shape=[jax.ShapeDtypeStruct(grad.shape, f32)] * 2,
        compiler_params=params(),
        name="settle",
    )(home, grad, state, back)


def hidden_kernel(
    core_ref,
    h_lo_ref,
    h_hi_ref,
    g_ref,
    scale_ref,
    mine_ref,
    theirs_ref,
    b1_ref,
    h_ref,
    df_ref,
    m_ref,
    du_ref,
    lo_ref,
    hi_ref,
    f_lo_ref,
    f_hi_ref,
    du_sum_ref,
    f_sum_ref,
    w_ref,
):
    step = pl.program_id(0)
    model = h_lo_ref.shape[1]
    width = w_ref.shape[1]
    w1 = w_ref.at[:model]
    w2 = [w_ref.at[model + n : model + n + width] for n in range(0, model, width)]

    @pl.when(step == 0)
    def _():
        w_ref[...] = jnp.where(core_ref[1] == 1, mine_ref[...], theirs_ref[...])

    h = from_halves(h_lo_ref, h_hi_ref)
    h_ref[...] = h
    gy = jnp.concatenate([g_ref[n, 0] for n in range(g_ref.shape[0])], 0).astype(f32)
    df = (gy * scale_ref[...]).astype(bf16)
    df_ref[...] = df
    u = dot_nn(h, w1[...]) + b1_ref[...]
    phi = 0.5 * (1.0 + lax.erf(u * inv_root_two))
    m = (u * phi).astype(bf16)
    m_ref[...] = m
    dm = None
    for n, part in enumerate(w2):
        piece = dot_nt(df[:, n * width : (n + 1) * width], part[...])
        dm = piece if dm is None else dm + piece
    du = (dm * (phi + u * jnp.exp(-0.5 * u * u) * inv_root_two_pi)).astype(bf16)
    du_ref[...] = du
    to_halves(dot_nt(du, w1[...]).astype(bf16), lo_ref, hi_ref)
    f = jnp.concatenate([dot_nn(m, part[...]) for part in w2], 1)
    to_halves(f.astype(bf16), f_lo_ref, f_hi_ref)

    @pl.when(step == 0)
    def _():
        du_sum_ref[...] = jnp.zeros_like(du_sum_ref)
        f_sum_ref[...] = jnp.zeros_like(f_sum_ref)

    du_sum_ref[0:1, :] += jnp.sum(du.astype(f32), 0, keepdims=True)
    f_sum_ref[0:1, :] += jnp.sum(gy * f, 0, keepdims=True)


def hidden_block(core, h_lo, h_hi, g, scale, mine, theirs, b1):
    rows, model = 2 * h_lo.shape[0], h_lo.shape[1]
    width = mine.shape[1]
    blocks = rows // BLOCK
    each = BLOCK // g.shape[2]
    like = jax.ShapeDtypeStruct
    return pl.pallas_call(
        hidden_kernel,
        grid_spec=pltpu.PrefetchScalarGridSpec(
            num_scalar_prefetch=1,
            grid=(blocks,),
            in_specs=half_specs(model, blocks)
            + [
                pl.BlockSpec(
                    (each, 1) + g.shape[2:],
                    lambda i, core: ((i + core[0] * (blocks // 2)) % blocks, 1, 0, 0),
                ),
                whole((1, model)),
                whole(mine.shape),
                whole(mine.shape),
                whole((1, width)),
            ],
            out_specs=[
                rows_of(model),
                rows_in_order(model, blocks),
                rows_in_order(width, blocks),
                rows_of(width),
                whole((rows // 2, model)),
                whole((rows // 2, model)),
                whole((rows // 2, model)),
                whole((rows // 2, model)),
                whole((8, width)),
                whole((8, model)),
            ],
            scratch_shapes=[pltpu.VMEM(mine.shape, bf16)],
        ),
        out_shape=[
            like((rows, model), bf16),
            like((rows, model), bf16),
            like((rows, width), bf16),
            like((rows, width), bf16),
            like((rows // 2, model), bf16),
            like((rows // 2, model), bf16),
            like((rows // 2, model), bf16),
            like((rows // 2, model), bf16),
            like((8, width), f32),
            like((8, model), f32),
        ],
        compiler_params=params(40),
        name="hidden_block",
    )(core, h_lo, h_hi, g, scale, mine, theirs, b1)


def project_back_kernel(
    dq_ref, dk_ref, dv_ref, w_ref, x_lo_ref, x_hi_ref, early_ref, lo_ref, hi_ref, fold_ref, sum_ref
):
    step = pl.program_id(0)
    last = pl.num_programs(0) - 1
    dh = dot_nt(dq_ref[...], w_ref[0]) + dot_nt(dk_ref[...], w_ref[1]) + dot_nt(dv_ref[...], w_ref[2])
    normed, _ = norm_pieces(from_halves(x_lo_ref, x_hi_ref).astype(f32))

    @pl.when(step == 0)
    def _():
        sum_ref[...] = early_ref[...]

    to_halves(dh.astype(bf16), lo_ref, hi_ref)
    sum_ref[0:1, :] += jnp.sum(dh * normed, 0, keepdims=True)
    sum_ref[1:2, :] += jnp.sum(dh, 0, keepdims=True)

    @pl.when(step == last)
    def _():
        width = fold_ref.shape[1]
        for n in range(sum_ref.shape[1] // width):
            fold_ref[8 * n : 8 * n + 8, :] = sum_ref[0:8, n * width : (n + 1) * width]


def project_back(dq, dk, dv, w, x_lo, x_hi, early):
    rows, model = 2 * x_lo.shape[0], x_lo.shape[1]
    width = dq.shape[1]
    half = (rows // 2, model)
    folded = (8 * model // width, width)
    return pl.pallas_call(
        project_back_kernel,
        grid=(rows // BLOCK,),
        in_specs=[rows_of(width)] * 3
        + [whole(w.shape)]
        + half_specs(model, rows // BLOCK)
        + [whole((16, model))],
        out_specs=[whole(half), whole(half), whole(folded)],
        out_shape=[
            jax.ShapeDtypeStruct(half, bf16),
            jax.ShapeDtypeStruct(half, bf16),
            jax.ShapeDtypeStruct(folded, f32),
        ],
        scratch_shapes=[pltpu.VMEM((16, model), f32)],
        compiler_params=params(),
        name="project_back",
    )(dq, dk, dv, w, x_lo, x_hi, early)


AXES = ("dp", "tensor")


def members(key):
    found = {}
    for core in range(2):
        for z in range(4):
            for y in range(4):
                for xh in range(2):
                    for xl in range(2):
                        found.setdefault(key(xh, xl, y, z, core), []).append(
                            ((xl * 4 + y) * 2 + core) * 8 + xh * 4 + z
                        )
    return list(found.values())


def links(move):
    pairs = []
    for xh in range(2):
        for xl in range(2):
            for y in range(4):
                for z in range(4):
                    for core in range(2):
                        there = move(xh, xl, y, z, core)
                        if there is None:
                            continue
                        ph, pl_, py, pz, pc = there
                        pairs.append(
                            (
                                ((xl * 4 + y) * 2 + core) * 8 + xh * 4 + z,
                                ((pl_ * 4 + py % 4) * 2 + pc) * 8 + ph * 4 + pz % 4,
                            )
                        )
    return pairs


z_up = links(lambda xh, xl, y, z, c: (xh, xl, y, z + 1, c))
z_down = links(lambda xh, xl, y, z, c: (xh, xl, y, z - 1, c))
z_far = links(lambda xh, xl, y, z, c: (xh, xl, y, z + 2, c))
y_up = links(lambda xh, xl, y, z, c: (xh, xl, y + 1, z, c))
y_down = links(lambda xh, xl, y, z, c: (xh, xl, y - 1, z, c))
y_far = links(lambda xh, xl, y, z, c: (xh, xl, y + 2, z, c))
x_far = links(lambda xh, xl, y, z, c: (1 - xh, xl, y, z, c))
x_near = links(lambda xh, xl, y, z, c: (xh, 1 - xl, y, z, c))
cores = links(lambda xh, xl, y, z, c: (xh, xl, y, z, 1 - c))
regroup = links(lambda xh, xl, y, z, c: (c, xl, y, z, xh) if xh != c else None)
home = links(lambda xh, xl, y, z, c: (c, xl, y, z, c) if xh != c else None)
ring_z = members(lambda xh, xl, y, z, c: (xh, xl, y, c))
ring_y = members(lambda xh, xl, y, z, c: (xh, xl, z, c))
image = members(lambda xh, xl, y, z, c: (xh, xl, y))


def move(values, pairs):
    return lax.ppermute(values, AXES, pairs)


def exchange(values, groups):
    return lax.all_to_all(values, AXES, 0, 0, axis_index_groups=groups, tiled=True)


def gather(values, groups):
    return lax.all_gather(values, AXES, axis=0, axis_index_groups=groups, tiled=True)


def ring_from(values, up, down, far):
    return [values, move(values, down), move(values, up), move(values, far)]


def spread(rows):
    half = exchange(jnp.concatenate([rows] * 4, 0), ring_z)
    return half, move(half, cores)


def terms(values):
    first = lax.reduce_precision(values, 8, 7)
    rest = values - first
    second = lax.reduce_precision(rest, 8, 7)
    return low(jnp.concatenate([first, second, rest - second], 0))


def after(values, *others):
    return lax.optimization_barrier((values, *others))[0]


def wide(values):
    return values.astype(f32)


def low(values):
    return values.astype(bf16)


def turn(values, axis, start):
    return lax.dynamic_slice_in_dim(jnp.concatenate([values, values], axis), start % 4, 4, axis)


def unfold(values, rows):
    return jnp.concatenate([values[n : n + rows] for n in range(0, values.shape[0], rows)], 1)


def at_home(here, there, home_here):
    return jnp.where(home_here, here, there), jnp.where(home_here, there, here)


def shards(
    tokens,
    cotangent,
    w_qkv,
    qv_bias,
    w_out,
    w_fc1,
    b_fc1,
    w_fc2,
    norm_gain,
    norm_shift,
    out_bias,
    layer_scale,
):
    layer = 0
    place = lax.axis_index("dp")
    core = place % 2
    y = (place // 2) % 4
    x_hi = lax.axis_index("tensor") // 4
    z = lax.axis_index("tensor") % 4
    home_here = x_hi == core
    core_arg = core.astype(jnp.int32).reshape(1)
    home_arg = home_here.astype(jnp.int32).reshape(1)
    width = w_qkv.shape[3]
    hidden_here = w_fc1.shape[2]
    own, model = tokens.shape

    def regrouped(values):
        return jnp.where(home_here, values, move(values, regroup))

    rows_in = regrouped(tokens)
    bias_terms = terms(jnp.concatenate([qv_bias[layer].reshape(-1, width), b_fc1.reshape(-1, width)], 0))
    bias_rows = bias_terms.shape[0]
    bias_terms = jnp.pad(bias_terms, ((0, -bias_rows % 16), (0, 0)))
    first = pack(jnp.moveaxis(w_qkv[layer], 1, 0), w_out[layer], cotangent, bias_terms)
    first_got = move(after(first, rows_in), regroup)
    tokens_lo = exchange(jnp.concatenate([rows_in] * 4, 0), ring_z)
    fc_mine = jnp.concatenate(
        [w_fc1[layer], w_fc2[layer][:, :hidden_here], w_fc2[layer][:, hidden_here:]], 0
    )
    first_got, tokens_lo, fc_mine = lax.optimization_barrier((first_got, tokens_lo, fc_mine))
    tokens_hi = move(tokens_lo, cores)
    qkv_in, out_grad, biases = unpack(
        home_arg, first, first_got, 3, model, bias_terms.shape[0]
    )
    biases = jnp.sum(wide(biases[:bias_rows]).reshape(3, -1, width), 0)
    qv_in = biases[:2]
    hidden_bias = biases[2:].reshape(1, hidden_here)
    out_grad_full = gather(out_grad.reshape(2 * own, model), image).reshape(8, 2, own, model)

    normed_full, query_rows, key_rows, value_rows = project(
        tokens_lo, tokens_hi, norm_gain[layer, 0:1], norm_shift[layer, 0:1], qkv_in, qv_in
    )
    mixed, mixed_own, log_total = attend(core_arg, query_rows, key_rows, value_rows)
    pieces = exchange(mixed, image).reshape(8, own, width)
    fc_got = move(after(fc_mine, pieces), regroup)
    sent_two, branch, middle = middle_rows(
        pieces,
        out_grad_full,
        rows_in,
        out_bias[layer, 0:1],
        layer_scale[layer, 0:1],
        norm_gain[layer, 1:2],
        norm_shift[layer, 1:2],
    )
    two_lo = exchange(sent_two, ring_z).reshape(4 * own, model)
    two_hi = move(two_lo, cores)
    half = two_lo.shape[0]

    normed_two_full, down_full, hidden, act_grad, lo_two, hi_two, f_lo, f_hi, du_sums, f_sums = (
        hidden_block(
            jnp.concatenate([core_arg, home_arg]),
            two_lo,
            two_hi,
            out_grad_full,
            layer_scale[layer, 1:2],
            fc_mine,
            fc_got,
            hidden_bias,
        )
    )
    mine_two = low(wide(lo_two) + wide(move(hi_two, cores)))
    got_two = exchange(mine_two.reshape(4, own, model), ring_z)
    grad_b1 = du_sums[0]

    grad_fc2 = jnp.einsum("gf,gd->fd", hidden, down_full, preferred_element_type=f32)
    grad_fc1 = jnp.einsum("gd,gf->df", normed_two_full, act_grad, preferred_element_type=f32)
    joined = jnp.concatenate(
        [low(grad_fc1), low(grad_fc2[:, : model // 2]), low(grad_fc2[:, model // 2 :])], 0
    )
    joined, got_two = lax.optimization_barrier((joined, got_two))
    fc_quarter_y = lax.psum_scatter(
        joined, AXES, scatter_dimension=0, axis_index_groups=ring_y, tiled=True
    )
    gradient_two, sent, early = middle_back(
        core_arg,
        got_two,
        middle,
        branch,
        out_grad,
        norm_gain[layer, 1:2],
        layer_scale[layer],
        out_bias[layer, 1:2],
        out_grad_full,
        f_sums,
        width,
    )
    back_lo = exchange(sent, ring_z).reshape(4 * own, model + 2 * width)
    back_hi = move(back_lo[:, : model + width], cores)
    query_grad, key_grad, value_grad, qv_sums = attend_back(
        query_rows,
        key_rows,
        value_rows,
        back_lo,
        (model + width) // width,
        back_hi,
        model // width,
        log_total,
    )
    fc_quarter = low(wide(fc_quarter_y) + wide(move(fc_quarter_y, x_near)))
    query_grad, fc_quarter = lax.optimization_barrier((query_grad, fc_quarter))
    lo, hi, small = project_back(
        query_grad, key_grad, value_grad, qkv_in, tokens_lo, tokens_hi, early
    )
    small_here, small_above, small_below, small_across = [
        wide(piece) for piece in ring_from(low(small), z_up, z_down, z_far)
    ]
    small = (small_here + small_across) + (small_above + small_below)
    payload = weight_grads(
        normed_full, after(query_grad, lo), key_grad, value_grad, mixed_own, back_lo, back_hi
    )
    fc_quarter = low(wide(fc_quarter) + wide(move(fc_quarter, x_far)))
    rows_joined = join_rows(lo, f_lo, move(hi, cores), move(f_hi, cores))

    quarter = payload.shape[0] // 4
    got_q = exchange(payload, ring_y)
    got_q, fc_quarter, rows_joined = lax.optimization_barrier((got_q, fc_quarter, rows_joined))
    got = exchange(rows_joined, ring_z)
    rows_q = jnp.sum(wide(got_q).reshape(4, quarter, width), 0)
    wide_bias = jnp.concatenate(
        [qv_sums[:2].reshape(-1), grad_b1, jnp.zeros((model - 2 * width - hidden_here,), f32)]
    )
    wide_bias = jnp.concatenate([wide_bias, jnp.zeros_like(wide_bias)]).reshape(-1, width)
    flow = jnp.concatenate([low(rows_q), low(small), low(wide_bias)], 0)
    flow = low(wide(flow) + wide(move(flow, x_far)))
    fc_half = fc_quarter.shape[0] // 2
    fc_part = jnp.where(home_here, fc_quarter[:fc_half], move(fc_quarter[fc_half:], cores))
    flow = low(wide(flow) + wide(move(flow, x_near)))
    flow, fc_part = lax.optimization_barrier((flow, fc_part))
    fc_all = gather(fc_part, ring_y).reshape(4, fc_half, -1)
    fine = quarter // 2
    kept = jnp.where(home_here, flow[:fine], move(flow[fine:quarter], cores))
    sent_y = jnp.concatenate([kept, flow[quarter:]], 0)
    gradient_one, state_one, rows_sent = last_rows(
        got,
        rows_in,
        gradient_two,
        norm_gain[layer, 0:1],
        middle,
        out_bias[layer, 1:2],
        layer_scale[layer, 1:2],
    )
    rows_back = move(rows_sent, regroup)
    got_y = ring_from(sent_y, y_up, y_down, y_far)
    (here, above, below, across), rows_back = lax.optimization_barrier((tuple(got_y), rows_back))
    gradient_out, state_out = settle(home_arg, gradient_one, state_one, rows_back)
    extra = flow.shape[0] - quarter
    block = block_rows(extra, here, above, below, across)
    tail = block[4 * fine :]
    other = move(block, cores)
    small_rows = small.shape[0]
    small = wide(tail[:small_rows]) + wide(other[4 * fine : 4 * fine + small_rows])
    small_total = unfold(small, 8)
    total_qkv, total_out = finish(
        jnp.concatenate([home_arg, y.astype(jnp.int32).reshape(1)]), block, other, model
    )
    total_qkv = jnp.moveaxis(total_qkv, 0, 1)
    total_fc1, total_fc2 = finish_hidden(home_arg, fc_all, move(fc_all, cores), model)
    bias_rows_mine = jnp.where(home_here, tail[small_rows:], other[4 * fine + small_rows :])
    bias_total = wide(bias_rows_mine).reshape(2, model)[:1]
    return (
        state_out,
        gradient_out,
        total_qkv[None],
        bias_total[:, : 2 * width].reshape(1, 2, width),
        total_out[None],
        total_fc1[None],
        bias_total[:, 2 * width : 2 * width + hidden_here],
        total_fc2[None],
        jnp.stack([small_total[0], small_total[2]])[None],
        jnp.stack([small_total[1], small_total[3]])[None],
        small_total[4:6][None],
        small_total[6:8][None],
    )


def solution(mesh):
    return jax.shard_map(
        shards,
        mesh=mesh,
        in_specs=(
            P(("dp", "tensor"), None),
            P(("dp", "tensor"), None),
            P(None, None, None, "tensor"),
            P(None, None, "tensor"),
            P(None, "tensor", None),
            P(None, None, "tensor"),
            P(None, "tensor"),
            P(None, "tensor", None),
            P(),
            P(),
            P(),
            P(),
        ),
        out_specs=(
            P(("dp", "tensor"), None),
            P(("dp", "tensor"), None),
            P(None, None, None, "tensor"),
            P(None, None, "tensor"),
            P(None, "tensor", None),
            P(None, None, "tensor"),
            P(None, "tensor"),
            P(None, "tensor", None),
            P(),
            P(),
            P(),
            P(),
        ),
        check_vma=False,
    )
```

```python
import functools

import jax
import jax.numpy as jnp
from jax import lax
from jax.experimental import pallas as pl
from jax.experimental.pallas import tpu as pltpu
from jax.sharding import PartitionSpec as P

HD = 64
BLOCK = 256
inv_root_two = 0.7071067811865476
inv_root_two_pi = 0.3989422804014327
f32 = jnp.float32
bf16 = jnp.bfloat16


def dot_nn(a, b):
    return lax.dot_general(a, b, (((1,), (0,)), ((), ())), preferred_element_type=f32)


def dot_nt(a, b):
    return lax.dot_general(a, b, (((1,), (1,)), ((), ())), preferred_element_type=f32)


def params(mebibytes=24):
    return pltpu.CompilerParams(vmem_limit_bytes=mebibytes * 1024 * 1024)


def whole(shape):
    return pl.BlockSpec(shape, lambda i, *_: (0,) * len(shape))


def rows_of(width, block=BLOCK):
    return pl.BlockSpec((block, width), lambda i, *_: (i, 0))


def rows_in_order(width, blocks):
    return pl.BlockSpec((BLOCK, width), lambda i, core: ((i + core[0] * (blocks // 2)) % blocks, 0))


def half_specs(width, blocks):
    half = blocks // 2
    return [
        pl.BlockSpec((BLOCK, width), lambda i, *_: (jnp.minimum(i, half - 1), 0)),
        pl.BlockSpec((BLOCK, width), lambda i, *_: (jnp.maximum(i - half, 0), 0)),
    ]


def from_halves(lo_ref, hi_ref):
    return jnp.where(pl.program_id(0) < pl.num_programs(0) // 2, lo_ref[...], hi_ref[...])


def to_halves(values, lo_ref, hi_ref):
    step = pl.program_id(0)
    half = pl.num_programs(0) // 2

    @pl.when(step < half)
    def _():
        lo_ref[pl.ds(pl.multiple_of(step * BLOCK, BLOCK), BLOCK), :] = values

    @pl.when(step >= half)
    def _():
        hi_ref[pl.ds(pl.multiple_of((step - half) * BLOCK, BLOCK), BLOCK), :] = values


def norm_pieces(values):
    centred = values - jnp.mean(values, -1, keepdims=True)
    inv_dev = lax.rsqrt(jnp.mean(centred * centred, -1, keepdims=True) + 1e-06)
    return centred * inv_dev, inv_dev


def project_kernel(lo_ref, hi_ref, gain_ref, shift_ref, w_ref, bias_ref, h_ref, q_ref, k_ref, v_ref):
    normed, _ = norm_pieces(from_halves(lo_ref, hi_ref).astype(f32))
    h = (normed * gain_ref[...] + shift_ref[...]).astype(bf16)
    h_ref[...] = h
    q_ref[...] = (dot_nn(h, w_ref[0]) + bias_ref[0:1, :]).astype(bf16)
    k_ref[...] = dot_nn(h, w_ref[1]).astype(bf16)
    v_ref[...] = (dot_nn(h, w_ref[2]) + bias_ref[1:2, :]).astype(bf16)


def project(lo, hi, gain, shift, w, bias):
    rows, model = 2 * lo.shape[0], lo.shape[1]
    width = w.shape[2]
    out = jax.ShapeDtypeStruct((rows, width), bf16)
    return pl.pallas_call(
        project_kernel,
        grid=(rows // BLOCK,),
        in_specs=half_specs(model, rows // BLOCK)
        + [whole((1, model)), whole((1, model)), whole(w.shape), whole(bias.shape)],
        out_specs=[rows_of(model)] + [rows_of(width)] * 3,
        out_shape=[jax.ShapeDtypeStruct((rows, model), bf16), out, out, out],
        compiler_params=params(),
        name="norm_project",
    )(lo, hi, gain, shift, w, bias)


def lane_mask(shape, head, dim):
    return (lax.broadcasted_iota(jnp.int32, shape, dim) // HD) == head


def only_head(values, head, dim=1):
    return jnp.where(lane_mask(values.shape, head, dim), values, jnp.zeros_like(values))


def attend_kernel(core_ref, q_ref, k_ref, v_ref, o_ref, own_ref, lse_ref):
    q = q_ref[...] * jnp.asarray(HD**-0.5, bf16)
    v_t = v_ref[...].T
    total = None
    for head in range(q.shape[1] // HD):
        scores = dot_nt(k_ref[...], only_head(q, head))
        top = jnp.max(scores, 0, keepdims=True)
        shifted = jnp.exp(scores - top)
        row_sum = jnp.sum(shifted, 0, keepdims=True)
        prob = (shifted * (1.0 / row_sum)).astype(bf16)
        lse_ref[head : head + 1, :] = top + jnp.log(row_sum)
        piece = dot_nn(only_head(v_t, head, 0), prob)
        total = piece if total is None else total + piece
    o = total.astype(bf16).T
    o_ref[...] = o
    own_ref[...] = o


def attend(core, q, k, v):
    rows, width = q.shape
    heads = width // HD
    return pl.pallas_call(
        attend_kernel,
        grid_spec=pltpu.PrefetchScalarGridSpec(
            num_scalar_prefetch=1,
            grid=(rows // BLOCK,),
            in_specs=[rows_of(width), whole(k.shape), whole(v.shape)],
            out_specs=[
                rows_in_order(width, rows // BLOCK),
                rows_of(width),
                pl.BlockSpec((heads, BLOCK), lambda i, *_: (0, i)),
            ],
        ),
        out_shape=[jax.ShapeDtypeStruct((rows, width), bf16)] * 2 + [jax.ShapeDtypeStruct((heads, rows), f32)],
        compiler_params=params(),
        name="attend",
    )(core, q, k, v)


def attend_back_kernel(
    q_ref,
    do_lo_ref,
    do_hi_ref,
    lse_ref,
    k_ref,
    v_ref,
    dq_ref,
    dk_ref,
    dv_ref,
    sum_ref,
    dk_acc,
    dv_acc,
):
    step = pl.program_id(0)
    last = pl.num_programs(0) - 1
    scale = HD**-0.5

    @pl.when(step == 0)
    def _():
        dk_acc[...] = jnp.zeros_like(dk_acc)
        dv_acc[...] = jnp.zeros_like(dv_acc)
        sum_ref[...] = jnp.zeros_like(sum_ref)

    q = q_ref[...] * jnp.asarray(scale, bf16)
    do = from_halves(do_lo_ref, do_hi_ref)
    k_t = k_ref[...].T
    dq_t = None
    for head in range(q.shape[1] // HD):
        q_h = only_head(q, head)
        do_h = only_head(do, head)
        prob = jnp.exp(dot_nt(k_ref[...], q_h) - lse_ref[head : head + 1, :])
        d_prob = dot_nt(v_ref[...], do_h)
        row = jnp.sum(d_prob * prob, 0, keepdims=True)
        d_score = (prob * (d_prob - row)).astype(bf16)
        dv_acc[...] += dot_nn(prob.astype(bf16), do_h)
        dk_acc[...] += dot_nn(d_score, q_h)
        piece = dot_nn(only_head(k_t, head, 0), d_score)
        dq_t = piece if dq_t is None else dq_t + piece
    dq = (dq_t * scale).astype(bf16).T
    dq_ref[...] = dq
    sum_ref[0:1, :] += jnp.sum(dq.astype(f32), 0, keepdims=True)

    @pl.when(step == last)
    def _():
        dk_ref[...] = dk_acc[...].astype(bf16)
        dv = dv_acc[...].astype(bf16)
        dv_ref[...] = dv
        sum_ref[1:2, :] = jnp.sum(dv.astype(f32), 0, keepdims=True)


def attend_back(q, k, v, do_lo, lo_block, do_hi, hi_block, lse):
    rows, width = q.shape
    heads = width // HD
    half = rows // BLOCK // 2
    out = jax.ShapeDtypeStruct((rows, width), bf16)
    return pl.pallas_call(
        attend_back_kernel,
        grid=(rows // BLOCK,),
        in_specs=[
            rows_of(width),
            pl.BlockSpec((BLOCK, width), lambda i: (jnp.minimum(i, half - 1), lo_block)),
            pl.BlockSpec((BLOCK, width), lambda i: (jnp.maximum(i - half, 0), hi_block)),
            pl.BlockSpec((heads, BLOCK), lambda i: (0, i)),
            whole(k.shape),
            whole(v.shape),
        ],
        out_specs=[rows_of(width), whole(k.shape), whole(v.shape), whole((8, width))],
        out_shape=[out, out, out, jax.ShapeDtypeStruct((8, width), f32)],
        scratch_shapes=[pltpu.VMEM((rows, width), f32), pltpu.VMEM((rows, width), f32)],
        compiler_params=params(),
        name="attend_back",
    )(q, do_lo, do_hi, lse, k, v)


def pack_kernel(qkv_ref, out_ref, grad_ref, bias_ref, pack_ref):
    parts, rows, width = qkv_ref.shape
    for n in range(parts):
        pack_ref[n * rows : (n + 1) * rows, :] = qkv_ref[n]
    start = parts * rows
    for ref in (out_ref, grad_ref):
        for n in range(ref.shape[1] // width):
            pack_ref[start : start + width, :] = ref[:, n * width : (n + 1) * width]
            start += width
    pack_ref[start:, :] = bias_ref[...]


def pack(qkv, out, grad, bias):
    width = qkv.shape[2]
    rows = qkv.shape[0] * qkv.shape[1] + 2 * out.shape[1] + bias.shape[0]
    return pl.pallas_call(
        pack_kernel,
        out_shape=jax.ShapeDtypeStruct((rows, width), bf16),
        compiler_params=params(),
        name="pack",
    )(qkv, out, grad, bias)


def unpack_kernel(home_ref, mine_ref, got_ref, qkv_ref, both_ref, bias_ref):
    parts, rows, width = qkv_ref.shape
    first = home_ref[0] == 1
    pick = lambda start, size: jnp.where(
        first, mine_ref[start : start + size, :], got_ref[start : start + size, :]
    )
    for n in range(parts):
        qkv_ref[n] = pick(n * rows, rows)
    start = parts * rows
    for half in range(2):
        for n in range(both_ref.shape[2] // width):
            both_ref[half, :, n * width : (n + 1) * width] = pick(start, width)
            start += width
    bias_ref[...] = pick(start, bias_ref.shape[0])


def unpack(home, mine, got, parts, model, bias_rows):
    width = mine.shape[1]
    like = jax.ShapeDtypeStruct
    vmem = pl.BlockSpec(memory_space=pltpu.VMEM)
    return pl.pallas_call(
        unpack_kernel,
        in_specs=[pl.BlockSpec(memory_space=pltpu.SMEM), vmem, vmem],
        out_shape=[
            like((parts, model, width), bf16),
            like((2, width, model), bf16),
            like((bias_rows, width), bf16),
        ],
        compiler_params=params(),
        name="unpack",
    )(home, mine, got)


def middle_kernel(pieces_ref, w_ref, x_ref, bias_ref, scale_ref, gain_ref, shift_ref, sent_ref, a_ref, x1_ref):
    o = jnp.concatenate([pieces_ref[n] for n in range(pieces_ref.shape[0])], 1)
    w = jnp.concatenate([w_ref[n, 0] for n in range(w_ref.shape[0])], 0)
    a = dot_nn(o, w) + bias_ref[...]
    a_ref[...] = a
    x1 = x_ref[...].astype(f32) + scale_ref[...] * a
    x1_ref[...] = x1
    normed, _ = norm_pieces(x1)
    h = (normed * gain_ref[...] + shift_ref[...]).astype(bf16)
    for n in range(4):
        sent_ref[n] = h


def first_of_pairs(pairs):
    return pl.BlockSpec((pairs.shape[0], 1) + pairs.shape[2:], lambda i, *_: (0, 0, 0, 0))


def middle_rows(pieces, w, x, bias, scale, gain, shift):
    rows, model = x.shape
    like = jax.ShapeDtypeStruct
    return pl.pallas_call(
        middle_kernel,
        grid=(1,),
        in_specs=[whole(pieces.shape), first_of_pairs(w)]
        + [whole(v.shape) for v in (x, bias, scale, gain, shift)],
        out_specs=[whole((4, rows, model)), whole((rows, model)), whole((rows, model))],
        out_shape=[like((4, rows, model), bf16), like((rows, model), f32), like((rows, model), f32)],
        compiler_params=params(48),
        name="middle_rows",
    )(pieces, w, x, bias, scale, gain, shift)


def norm_back(upstream, normed, inv_dev, gain):
    scaled = upstream * gain
    return inv_dev * (
        scaled
        - jnp.mean(scaled, -1, keepdims=True)
        - normed * jnp.mean(scaled * normed, -1, keepdims=True)
    )


def norm_back_rows(upstream, values, gain):
    normed, inv_dev = norm_pieces(values)
    return normed, norm_back(upstream, normed, inv_dev, gain)


def middle_back_kernel(
    core_ref,
    got_ref,
    x1_ref,
    a_ref,
    gy_ref,
    gain_ref,
    scale_ref,
    bias_ref,
    w_ref,
    f_sum_ref,
    g1_ref,
    sent_ref,
    early_ref,
):
    total = lambda v: jnp.sum(v, 0, keepdims=True)
    dh2 = got_ref[0].astype(f32)
    for n in range(1, 4):
        dh2 = dh2 + got_ref[n].astype(f32)
    gy = gy_ref[0].astype(f32)
    normed, back = norm_back_rows(dh2, x1_ref[...], gain_ref[...])
    g1 = gy + back
    g1_ref[...] = g1
    da = (scale_ref[0:1, :] * g1).astype(bf16)
    w = jnp.concatenate([w_ref[n, 0] for n in range(w_ref.shape[0])], 0)
    do = dot_nt(da, w).astype(bf16)
    width = sent_ref.shape[2] - da.shape[1]
    first = core_ref[0] == 0
    half = da.shape[1] // 2
    piece = width // 2
    for n in range(4):
        low_part = do[:, n * piece : (n + 1) * piece]
        high_part = do[:, half + n * piece : half + (n + 1) * piece]
        sent_ref[n, :, : 2 * half] = da
        sent_ref[n, :, 2 * half : 2 * half + piece] = jnp.where(first, high_part, low_part)
        sent_ref[n, :, 2 * half + piece :] = jnp.where(first, low_part, high_part)
    early_ref[...] = jnp.zeros_like(early_ref)
    early_ref[2:3, :] = total(dh2 * normed)
    early_ref[3:4, :] = total(dh2)
    early_ref[4:5, :] = total(da.astype(f32))
    early_ref[5:6, :] = total((scale_ref[1:2, :] * gy).astype(bf16).astype(f32))
    early_ref[6:7, :] = total(g1 * a_ref[...])
    early_ref[7:8, :] = f_sum_ref[0:1, :] + bias_ref[...] * total(gy)


def middle_back(core, got, x1, a, gy, gain, scale, bias, w, f_sums, width):
    rows, model = x1.shape
    like = jax.ShapeDtypeStruct
    return pl.pallas_call(
        middle_back_kernel,
        grid_spec=pltpu.PrefetchScalarGridSpec(
            num_scalar_prefetch=1,
            grid=(1,),
            in_specs=[whole(v.shape) for v in (got, x1, a)]
            + [pl.BlockSpec((1,) + gy.shape[1:], lambda i, *_: (1, 0, 0))]
            + [whole(v.shape) for v in (gain, scale, bias)]
            + [first_of_pairs(w), whole(f_sums.shape)],
            out_specs=[
                whole((rows, model)),
                whole((4, rows, model + 2 * width)),
                whole((16, model)),
            ],
        ),
        out_shape=[
            like((rows, model), f32),
            like((4, rows, model + 2 * width), bf16),
            like((16, model), f32),
        ],
        compiler_params=params(48),
        name="middle_back",
    )(core, got, x1, a, gy, gain, scale, bias, w, f_sums)


def weight_kernel(h_ref, dq_ref, dk_ref, dv_ref, o_ref, da_lo_ref, da_hi_ref, out_ref, turned):
    @pl.when(pl.program_id(0) == 0)
    def _():
        for n, ref in enumerate((dq_ref, dk_ref, dv_ref, o_ref)):
            turned[n] = ref[...].T

    part = out_ref.shape[0] // 4
    for n in range(3):
        out_ref[n * part : (n + 1) * part, :] = dot_nn(turned[n], h_ref[...]).astype(bf16).T
    rows = da_lo_ref.shape[0]
    grad = dot_nn(turned[3, :, :rows], da_lo_ref[...]) + dot_nn(turned[3, :, rows:], da_hi_ref[...])
    width = out_ref.shape[1]
    for n in range(part // width):
        start = 3 * part + n * width
        out_ref[start : start + width, :] = grad[:, n * width : (n + 1) * width].astype(bf16)


def weight_grads(h, dq, dk, dv, o, da_lo, da_hi):
    rows, model = h.shape
    width = dq.shape[1]
    part = model // 4
    columns = lambda n: (0, n)
    return pl.pallas_call(
        weight_kernel,
        grid=(4,),
        in_specs=[pl.BlockSpec((rows, part), columns)]
        + [whole((rows, width))] * 4
        + [pl.BlockSpec((rows // 2, part), columns)] * 2,
        out_specs=pl.BlockSpec((4 * part, width), lambda n: (n, 0)),
        scratch_shapes=[pltpu.VMEM((4, width, rows), bf16)],
        out_shape=jax.ShapeDtypeStruct((16 * part, width), bf16),
        compiler_params=params(),
        name="weight_grads",
    )(h, dq, dk, dv, o, da_lo, da_hi)


def block_kernel(extra, here_ref, above_ref, below_ref, across_ref, out_ref):
    fine = here_ref.shape[0] - extra
    for n, ref in enumerate((here_ref, above_ref, across_ref, below_ref)):
        out_ref[n * fine : (n + 1) * fine, :] = ref[:fine, :]
    pair = lambda a, b: a[fine:, :].astype(f32) + b[fine:, :].astype(f32)
    total = pair(here_ref, across_ref) + pair(above_ref, below_ref)
    out_ref[4 * fine :, :] = total.astype(bf16)


def block_rows(extra, here, above, below, across):
    rows, width = here.shape
    return pl.pallas_call(
        functools.partial(block_kernel, extra),
        out_shape=jax.ShapeDtypeStruct((4 * (rows - extra) + extra, width), bf16),
        compiler_params=params(),
        name="block_rows",
    )(here, above, below, across)


def finish_kernel(place_ref, block_ref, other_ref, qkv_ref, out_ref):
    home = place_ref[0] == 1
    y = place_ref[1]
    parts, model, width = qkv_ref.shape
    part = model // 4
    fine = 2 * part
    for n in range(4):
        rows = slice(n * fine, (n + 1) * fine)
        mine, theirs = block_ref[rows, :].astype(f32), other_ref[rows, :].astype(f32)
        first, second = jnp.where(home, mine, theirs), jnp.where(home, theirs, mine)
        quarter = lax.rem(y + n, 4)
        at = pl.ds(pl.multiple_of(quarter * part, part), part)
        qkv_ref[0, at, :] = first[:part]
        qkv_ref[1, at, :] = first[part:]
        qkv_ref[2, at, :] = second[:part]
        for k in range(part // width):
            column = pl.multiple_of(quarter * part + k * width, width)
            out_ref[:, pl.ds(column, width)] = second[part + k * width : part + (k + 1) * width]


def finish(place, block, other, model):
    width = block.shape[1]
    like = jax.ShapeDtypeStruct
    vmem = pl.BlockSpec(memory_space=pltpu.VMEM)
    return pl.pallas_call(
        finish_kernel,
        in_specs=[pl.BlockSpec(memory_space=pltpu.SMEM), vmem, vmem],
        out_shape=[like((3, model, width), f32), like((width, model), f32)],
        compiler_params=params(),
        name="finish",
    )(place, block, other)


def finish_hidden_kernel(home_ref, mine_ref, theirs_ref, one_ref, two_ref):
    home = home_ref[0] == 1
    half, width = mine_ref.shape[1:]
    model = one_ref.shape[0]
    for n in range(4):
        mine, theirs = mine_ref[n].astype(f32), theirs_ref[n].astype(f32)
        for k, rows in enumerate((jnp.where(home, mine, theirs), jnp.where(home, theirs, mine))):
            start = (2 * n + k) * half
            if start < model:
                one_ref[start : start + half, :] = rows
            else:
                column, row = divmod(start - model, width)
                two_ref[row : row + half, column * width : (column + 1) * width] = rows


def finish_hidden(home, mine, theirs, model):
    width = mine.shape[2]
    like = jax.ShapeDtypeStruct
    vmem = pl.BlockSpec(memory_space=pltpu.VMEM)
    return pl.pallas_call(
        finish_hidden_kernel,
        in_specs=[pl.BlockSpec(memory_space=pltpu.SMEM), vmem, vmem],
        out_shape=[like((model, width), f32), like((width, model), f32)],
        compiler_params=params(),
        name="finish_hidden",
    )(home, mine, theirs)


def join_kernel(lo_ref, f_lo_ref, got_ref, f_got_ref, out_ref):
    rows = out_ref.shape[1] // 2
    for n in range(4):
        block = slice(n * rows, (n + 1) * rows)
        for half, (one, two) in enumerate(((lo_ref, got_ref), (f_lo_ref, f_got_ref))):
            total = one[block, :].astype(f32) + two[block, :].astype(f32)
            out_ref[n, half * rows : (half + 1) * rows, :] = total.astype(bf16)


def join_rows(lo, f_lo, got, f_got):
    rows, model = lo.shape
    return pl.pallas_call(
        join_kernel,
        out_shape=jax.ShapeDtypeStruct((4, rows // 2, model), bf16),
        compiler_params=params(),
        name="join_rows",
    )(lo, f_lo, got, f_got)


def last_kernel(
    got_ref, x_ref, g1_ref, gain_ref, x1_ref, bias_ref, scale_ref, grad_ref, state_ref, sent_ref
):
    rows = x_ref.shape[0]
    total = got_ref[0].astype(f32)
    for n in range(1, 4):
        total = total + got_ref[n].astype(f32)
    _, back = norm_back_rows(total[:rows], x_ref[...].astype(f32), gain_ref[...])
    grad = g1_ref[...] + back
    state = x1_ref[...] + scale_ref[...] * (total[rows:] + bias_ref[...])
    grad_ref[...] = grad
    state_ref[...] = state
    sent_ref[:rows, :] = grad.astype(bf16)
    sent_ref[rows:, :] = state.astype(bf16)


def last_rows(got, x, g1, gain, x1, bias, scale):
    rows, model = x.shape
    like = jax.ShapeDtypeStruct
    return pl.pallas_call(
        last_kernel,
        out_shape=[
            like((rows, model), f32),
            like((rows, model), f32),
            like((2 * rows, model), bf16),
        ],
        compiler_params=params(),
        name="last_rows",
    )(got, x, g1, gain, x1, bias, scale)


def settle_kernel(home_ref, grad_ref, state_ref, back_ref, grad_out_ref, state_out_ref):
    home = home_ref[0] == 1
    rows = grad_ref.shape[0]
    grad_out_ref[...] = jnp.where(home, grad_ref[...], back_ref[:rows, :].astype(f32))
    state_out_ref[...] = jnp.where(home, state_ref[...], back_ref[rows:, :].astype(f32))


def settle(home, grad, state, back):
    vmem = pl.BlockSpec(memory_space=pltpu.VMEM)
    return pl.pallas_call(
        settle_kernel,
        in_specs=[pl.BlockSpec(memory_space=pltpu.SMEM)] + [vmem] * 3,
        out_shape=[jax.ShapeDtypeStruct(grad.shape, f32)] * 2,
        compiler_params=params(),
        name="settle",
    )(home, grad, state, back)


def hidden_kernel(
    core_ref,
    h_lo_ref,
    h_hi_ref,
    g_ref,
    scale_ref,
    mine_ref,
    theirs_ref,
    b1_ref,
    h_ref,
    df_ref,
    m_ref,
    du_ref,
    lo_ref,
    hi_ref,
    f_lo_ref,
    f_hi_ref,
    du_sum_ref,
    f_sum_ref,
    w_ref,
):
    step = pl.program_id(0)
    model = h_lo_ref.shape[1]
    width = w_ref.shape[1]
    w1 = w_ref.at[:model]
    w2 = [w_ref.at[model + n : model + n + width] for n in range(0, model, width)]

    @pl.when(step == 0)
    def _():
        w_ref[...] = jnp.where(core_ref[1] == 1, mine_ref[...], theirs_ref[...])

    h = from_halves(h_lo_ref, h_hi_ref)
    h_ref[...] = h
    gy = jnp.concatenate([g_ref[n, 0] for n in range(g_ref.shape[0])], 0).astype(f32)
    df = (gy * scale_ref[...]).astype(bf16)
    df_ref[...] = df
    u = dot_nn(h, w1[...]) + b1_ref[...]
    phi = 0.5 * (1.0 + lax.erf(u * inv_root_two))
    m = (u * phi).astype(bf16)
    m_ref[...] = m
    dm = None
    for n, part in enumerate(w2):
        piece = dot_nt(df[:, n * width : (n + 1) * width], part[...])
        dm = piece if dm is None else dm + piece
    du = (dm * (phi + u * jnp.exp(-0.5 * u * u) * inv_root_two_pi)).astype(bf16)
    du_ref[...] = du
    to_halves(dot_nt(du, w1[...]).astype(bf16), lo_ref, hi_ref)
    f = jnp.concatenate([dot_nn(m, part[...]) for part in w2], 1)
    to_halves(f.astype(bf16), f_lo_ref, f_hi_ref)

    @pl.when(step == 0)
    def _():
        du_sum_ref[...] = jnp.zeros_like(du_sum_ref)
        f_sum_ref[...] = jnp.zeros_like(f_sum_ref)

    du_sum_ref[0:1, :] += jnp.sum(du.astype(f32), 0, keepdims=True)
    f_sum_ref[0:1, :] += jnp.sum(gy * f, 0, keepdims=True)


def hidden_block(core, h_lo, h_hi, g, scale, mine, theirs, b1):
    rows, model = 2 * h_lo.shape[0], h_lo.shape[1]
    width = mine.shape[1]
    blocks = rows // BLOCK
    each = BLOCK // g.shape[2]
    like = jax.ShapeDtypeStruct
    return pl.pallas_call(
        hidden_kernel,
        grid_spec=pltpu.PrefetchScalarGridSpec(
            num_scalar_prefetch=1,
            grid=(blocks,),
            in_specs=half_specs(model, blocks)
            + [
                pl.BlockSpec(
                    (each, 1) + g.shape[2:],
                    lambda i, core: ((i + core[0] * (blocks // 2)) % blocks, 1, 0, 0),
                ),
                whole((1, model)),
                whole(mine.shape),
                whole(mine.shape),
                whole((1, width)),
            ],
            out_specs=[
                rows_of(model),
                rows_in_order(model, blocks),
                rows_in_order(width, blocks),
                rows_of(width),
                whole((rows // 2, model)),
                whole((rows // 2, model)),
                whole((rows // 2, model)),
                whole((rows // 2, model)),
                whole((8, width)),
                whole((8, model)),
            ],
            scratch_shapes=[pltpu.VMEM(mine.shape, bf16)],
        ),
        out_shape=[
            like((rows, model), bf16),
            like((rows, model), bf16),
            like((rows, width), bf16),
            like((rows, width), bf16),
            like((rows // 2, model), bf16),
            like((rows // 2, model), bf16),
            like((rows // 2, model), bf16),
            like((rows // 2, model), bf16),
            like((8, width), f32),
            like((8, model), f32),
        ],
        compiler_params=params(40),
        name="hidden_block",
    )(core, h_lo, h_hi, g, scale, mine, theirs, b1)


def project_back_kernel(
    dq_ref, dk_ref, dv_ref, w_ref, x_lo_ref, x_hi_ref, early_ref, lo_ref, hi_ref, fold_ref, sum_ref
):
    step = pl.program_id(0)
    last = pl.num_programs(0) - 1
    dh = dot_nt(dq_ref[...], w_ref[0]) + dot_nt(dk_ref[...], w_ref[1]) + dot_nt(dv_ref[...], w_ref[2])
    normed, _ = norm_pieces(from_halves(x_lo_ref, x_hi_ref).astype(f32))

    @pl.when(step == 0)
    def _():
        sum_ref[...] = early_ref[...]

    to_halves(dh.astype(bf16), lo_ref, hi_ref)
    sum_ref[0:1, :] += jnp.sum(dh * normed, 0, keepdims=True)
    sum_ref[1:2, :] += jnp.sum(dh, 0, keepdims=True)

    @pl.when(step == last)
    def _():
        width = fold_ref.shape[1]
        for n in range(sum_ref.shape[1] // width):
            fold_ref[8 * n : 8 * n + 8, :] = sum_ref[0:8, n * width : (n + 1) * width]


def project_back(dq, dk, dv, w, x_lo, x_hi, early):
    rows, model = 2 * x_lo.shape[0], x_lo.shape[1]
    width = dq.shape[1]
    half = (rows // 2, model)
    folded = (8 * model // width, width)
    return pl.pallas_call(
        project_back_kernel,
        grid=(rows // BLOCK,),
        in_specs=[rows_of(width)] * 3
        + [whole(w.shape)]
        + half_specs(model, rows // BLOCK)
        + [whole((16, model))],
        out_specs=[whole(half), whole(half), whole(folded)],
        out_shape=[
            jax.ShapeDtypeStruct(half, bf16),
            jax.ShapeDtypeStruct(half, bf16),
            jax.ShapeDtypeStruct(folded, f32),
        ],
        scratch_shapes=[pltpu.VMEM((16, model), f32)],
        compiler_params=params(),
        name="project_back",
    )(dq, dk, dv, w, x_lo, x_hi, early)


AXES = ("dp", "tensor")


def members(key):
    found = {}
    for core in range(2):
        for z in range(4):
            for y in range(4):
                for xh in range(2):
                    for xl in range(2):
                        found.setdefault(key(xh, xl, y, z, core), []).append(
                            ((xl * 4 + y) * 2 + core) * 8 + xh * 4 + z
                        )
    return list(found.values())


def links(move):
    pairs = []
    for xh in range(2):
        for xl in range(2):
            for y in range(4):
                for z in range(4):
                    for core in range(2):
                        there = move(xh, xl, y, z, core)
                        if there is None:
                            continue
                        ph, pl_, py, pz, pc = there
                        pairs.append(
                            (
                                ((xl * 4 + y) * 2 + core) * 8 + xh * 4 + z,
                                ((pl_ * 4 + py % 4) * 2 + pc) * 8 + ph * 4 + pz % 4,
                            )
                        )
    return pairs


z_up = links(lambda xh, xl, y, z, c: (xh, xl, y, z + 1, c))
z_down = links(lambda xh, xl, y, z, c: (xh, xl, y, z - 1, c))
z_far = links(lambda xh, xl, y, z, c: (xh, xl, y, z + 2, c))
y_up = links(lambda xh, xl, y, z, c: (xh, xl, y + 1, z, c))
y_down = links(lambda xh, xl, y, z, c: (xh, xl, y - 1, z, c))
y_far = links(lambda xh, xl, y, z, c: (xh, xl, y + 2, z, c))
x_far = links(lambda xh, xl, y, z, c: (1 - xh, xl, y, z, c))
x_near = links(lambda xh, xl, y, z, c: (xh, 1 - xl, y, z, c))
cores = links(lambda xh, xl, y, z, c: (xh, xl, y, z, 1 - c))
regroup = links(lambda xh, xl, y, z, c: (c, xl, y, z, xh) if xh != c else None)
home = links(lambda xh, xl, y, z, c: (c, xl, y, z, c) if xh != c else None)
ring_z = members(lambda xh, xl, y, z, c: (xh, xl, y, c))
ring_y = members(lambda xh, xl, y, z, c: (xh, xl, z, c))
image = members(lambda xh, xl, y, z, c: (xh, xl, y))


def move(values, pairs):
    return lax.ppermute(values, AXES, pairs)


def exchange(values, groups):
    return lax.all_to_all(values, AXES, 0, 0, axis_index_groups=groups, tiled=True)


def gather(values, groups):
    return lax.all_gather(values, AXES, axis=0, axis_index_groups=groups, tiled=True)


def ring_from(values, up, down, far):
    return [values, move(values, down), move(values, up), move(values, far)]


def spread(rows):
    half = exchange(jnp.concatenate([rows] * 4, 0), ring_z)
    return half, move(half, cores)


def terms(values):
    first = lax.reduce_precision(values, 8, 7)
    rest = values - first
    second = lax.reduce_precision(rest, 8, 7)
    return low(jnp.concatenate([first, second, rest - second], 0))


def after(values, *others):
    return lax.optimization_barrier((values, *others))[0]


def wide(values):
    return values.astype(f32)


def low(values):
    return values.astype(bf16)


def turn(values, axis, start):
    return lax.dynamic_slice_in_dim(jnp.concatenate([values, values], axis), start % 4, 4, axis)


def unfold(values, rows):
    return jnp.concatenate([values[n : n + rows] for n in range(0, values.shape[0], rows)], 1)


def at_home(here, there, home_here):
    return jnp.where(home_here, here, there), jnp.where(home_here, there, here)


def shards(
    tokens,
    cotangent,
    w_qkv,
    qv_bias,
    w_out,
    w_fc1,
    b_fc1,
    w_fc2,
    norm_gain,
    norm_shift,
    out_bias,
    layer_scale,
):
    layer = 0
    place = lax.axis_index("dp")
    core = place % 2
    y = (place // 2) % 4
    x_hi = lax.axis_index("tensor") // 4
    z = lax.axis_index("tensor") % 4
    home_here = x_hi == core
    core_arg = core.astype(jnp.int32).reshape(1)
    home_arg = home_here.astype(jnp.int32).reshape(1)
    width = w_qkv.shape[3]
    hidden_here = w_fc1.shape[2]
    own, model = tokens.shape

    def regrouped(values):
        return jnp.where(home_here, values, move(values, regroup))

    rows_in = regrouped(tokens)
    bias_terms = terms(jnp.concatenate([qv_bias[layer].reshape(-1, width), b_fc1.reshape(-1, width)], 0))
    bias_rows = bias_terms.shape[0]
    bias_terms = jnp.pad(bias_terms, ((0, -bias_rows % 16), (0, 0)))
    first = pack(jnp.moveaxis(w_qkv[layer], 1, 0), w_out[layer], cotangent, bias_terms)
    first_got = move(after(first, rows_in), regroup)
    tokens_lo = exchange(jnp.concatenate([rows_in] * 4, 0), ring_z)
    fc_mine = jnp.concatenate(
        [w_fc1[layer], w_fc2[layer][:, :hidden_here], w_fc2[layer][:, hidden_here:]], 0
    )
    first_got, tokens_lo, fc_mine = lax.optimization_barrier((first_got, tokens_lo, fc_mine))
    tokens_hi = move(tokens_lo, cores)
    qkv_in, out_grad, biases = unpack(
        home_arg, first, first_got, 3, model, bias_terms.shape[0]
    )
    biases = jnp.sum(wide(biases[:bias_rows]).reshape(3, -1, width), 0)
    qv_in = biases[:2]
    hidden_bias = biases[2:].reshape(1, hidden_here)
    out_grad_full = gather(out_grad.reshape(2 * own, model), image).reshape(8, 2, own, model)

    normed_full, query_rows, key_rows, value_rows = project(
        tokens_lo, tokens_hi, norm_gain[layer, 0:1], norm_shift[layer, 0:1], qkv_in, qv_in
    )
    mixed, mixed_own, log_total = attend(core_arg, query_rows, key_rows, value_rows)
    pieces = exchange(mixed, image).reshape(8, own, width)
    fc_got = move(after(fc_mine, pieces), regroup)
    sent_two, branch, middle = middle_rows(
        pieces,
        out_grad_full,
        rows_in,
        out_bias[layer, 0:1],
        layer_scale[layer, 0:1],
        norm_gain[layer, 1:2],
        norm_shift[layer, 1:2],
    )
    two_lo = exchange(sent_two, ring_z).reshape(4 * own, model)
    two_hi = move(two_lo, cores)
    half = two_lo.shape[0]

    normed_two_full, down_full, hidden, act_grad, lo_two, hi_two, f_lo, f_hi, du_sums, f_sums = (
        hidden_block(
            jnp.concatenate([core_arg, home_arg]),
            two_lo,
            two_hi,
            out_grad_full,
            layer_scale[layer, 1:2],
            fc_mine,
            fc_got,
            hidden_bias,
        )
    )
    mine_two = low(wide(lo_two) + wide(move(hi_two, cores)))
    got_two = exchange(mine_two.reshape(4, own, model), ring_z)
    grad_b1 = du_sums[0]

    grad_fc2 = jnp.einsum("gf,gd->fd", hidden, down_full, preferred_element_type=f32)
    grad_fc1 = jnp.einsum("gd,gf->df", normed_two_full, act_grad, preferred_element_type=f32)
    joined = jnp.concatenate(
        [low(grad_fc1), low(grad_fc2[:, : model // 2]), low(grad_fc2[:, model // 2 :])], 0
    )
    joined, got_two = lax.optimization_barrier((joined, got_two))
    fc_quarter_y = lax.psum_scatter(
        joined, AXES, scatter_dimension=0, axis_index_groups=ring_y, tiled=True
    )
    gradient_two, sent, early = middle_back(
        core_arg,
        got_two,
        middle,
        branch,
        out_grad,
        norm_gain[layer, 1:2],
        layer_scale[layer],
        out_bias[layer, 1:2],
        out_grad_full,
        f_sums,
        width,
    )
    back_lo = exchange(sent, ring_z).reshape(4 * own, model + 2 * width)
    back_hi = move(back_lo[:, : model + width], cores)
    query_grad, key_grad, value_grad, qv_sums = attend_back(
        query_rows,
        key_rows,
        value_rows,
        back_lo,
        (model + width) // width,
        back_hi,
        model // width,
        log_total,
    )
    fc_quarter = low(wide(fc_quarter_y) + wide(move(fc_quarter_y, x_near)))
    query_grad, fc_quarter = lax.optimization_barrier((query_grad, fc_quarter))
    lo, hi, small = project_back(
        query_grad, key_grad, value_grad, qkv_in, tokens_lo, tokens_hi, early
    )
    small_here, small_above, small_below, small_across = [
        wide(piece) for piece in ring_from(low(small), z_up, z_down, z_far)
    ]
    small = (small_here + small_across) + (small_above + small_below)
    payload = weight_grads(
        normed_full, after(query_grad, lo), key_grad, value_grad, mixed_own, back_lo, back_hi
    )
    fc_quarter = low(wide(fc_quarter) + wide(move(fc_quarter, x_far)))
    rows_joined = join_rows(lo, f_lo, move(hi, cores), move(f_hi, cores))

    quarter = payload.shape[0] // 4
    got_q = exchange(payload, ring_y)
    got_q, rows_joined = lax.optimization_barrier((got_q, rows_joined))
    got = exchange(rows_joined, ring_z)
    rows_q = jnp.sum(wide(got_q).reshape(4, quarter, width), 0)
    wide_bias = jnp.concatenate(
        [qv_sums[:2].reshape(-1), grad_b1, jnp.zeros((model - 2 * width - hidden_here,), f32)]
    )
    wide_bias = jnp.concatenate([wide_bias, jnp.zeros_like(wide_bias)]).reshape(-1, width)
    flow = jnp.concatenate([low(rows_q), low(small), low(wide_bias)], 0)
    flow = low(wide(flow) + wide(move(flow, x_far)))
    flow, fc_quarter = lax.optimization_barrier((flow, fc_quarter))
    fc_half = fc_quarter.shape[0] // 2
    fc_part = jnp.where(home_here, fc_quarter[:fc_half], move(fc_quarter[fc_half:], cores))
    flow = low(wide(flow) + wide(move(flow, x_near)))
    flow, fc_part = lax.optimization_barrier((flow, fc_part))
    fc_all = gather(fc_part, ring_y).reshape(4, fc_half, -1)
    fine = quarter // 2
    kept = jnp.where(home_here, flow[:fine], move(flow[fine:quarter], cores))
    sent_y = jnp.concatenate([kept, flow[quarter:]], 0)
    gradient_one, state_one, rows_sent = last_rows(
        got,
        rows_in,
        gradient_two,
        norm_gain[layer, 0:1],
        middle,
        out_bias[layer, 1:2],
        layer_scale[layer, 1:2],
    )
    rows_back = move(rows_sent, regroup)
    got_y = ring_from(sent_y, y_up, y_down, y_far)
    (here, above, below, across), rows_back = lax.optimization_barrier((tuple(got_y), rows_back))
    gradient_out, state_out = settle(home_arg, gradient_one, state_one, rows_back)
    extra = flow.shape[0] - quarter
    block = block_rows(extra, here, above, below, across)
    tail = block[4 * fine :]
    other = move(block, cores)
    small_rows = small.shape[0]
    small = wide(tail[:small_rows]) + wide(other[4 * fine : 4 * fine + small_rows])
    small_total = unfold(small, 8)
    total_qkv, total_out = finish(
        jnp.concatenate([home_arg, y.astype(jnp.int32).reshape(1)]), block, other, model
    )
    total_qkv = jnp.moveaxis(total_qkv, 0, 1)
    total_fc1, total_fc2 = finish_hidden(home_arg, fc_all, move(fc_all, cores), model)
    bias_rows_mine = jnp.where(home_here, tail[small_rows:], other[4 * fine + small_rows :])
    bias_total = wide(bias_rows_mine).reshape(2, model)[:1]
    return (
        state_out,
        gradient_out,
        total_qkv[None],
        bias_total[:, : 2 * width].reshape(1, 2, width),
        total_out[None],
        total_fc1[None],
        bias_total[:, 2 * width : 2 * width + hidden_here],
        total_fc2[None],
        jnp.stack([small_total[0], small_total[2]])[None],
        jnp.stack([small_total[1], small_total[3]])[None],
        small_total[4:6][None],
        small_total[6:8][None],
    )


def solution(mesh):
    return jax.shard_map(
        shards,
        mesh=mesh,
        in_specs=(
            P(("dp", "tensor"), None),
            P(("dp", "tensor"), None),
            P(None, None, None, "tensor"),
            P(None, None, "tensor"),
            P(None, "tensor", None),
            P(None, None, "tensor"),
            P(None, "tensor"),
            P(None, "tensor", None),
            P(),
            P(),
            P(),
            P(),
        ),
        out_specs=(
            P(("dp", "tensor"), None),
            P(("dp", "tensor"), None),
            P(None, None, None, "tensor"),
            P(None, None, "tensor"),
            P(None, "tensor", None),
            P(None, None, "tensor"),
            P(None, "tensor"),
            P(None, "tensor", None),
            P(),
            P(),
            P(),
            P(),
        ),
        check_vma=False,
    )
```
